128 devices in a mesh: group: 4 (over z), head: 32 (over y, x, core).
Axes of the slice: x: 4, y: 4, z: 4, core: 2. Of those that a mesh axis runs over, the one named last changes fastest.
Arguments:
- mixer_input: bfloat16 [4096, 16384], P('group', 'head'), may hold values from -6 to 6
- gate_input: bfloat16 [4096, 16384], P('group', 'head'), may hold values from -6 to 6
- step_raw: float32 [4096, 256], P('group', 'head'), may hold values from -5 to 5
- state_proj: bfloat16 [2, 4096, 8, 256], P(None, 'group'), may hold values from -0.75 to 0.75
- decay_log: float32 [256], P('head'), may hold values from -6.2 to -2.3
- step_bias: float32 [256], P('head'), may hold values from -2 to 0.5
- skip_gain: float32 [256], P('head'), may hold values from 0.3 to 2
- norm_gain: float32 [16384], P('head'), may hold values from 0.5 to 1.5
- out_weight: bfloat16 [16384, 8192], P('head'), may hold values from -0.09375 to 0.09375
- residual: bfloat16 [4096, 8192], P('group', 'head'), may hold values from -6 to 6
- new_spans: int32 [8], P('group'), may hold values from 1 to 4
- hit_owner: int32 [8, 256], P('group', 'head'), may hold values from 0 to 3, as said below
- hit_slot: int32 [8, 256], P('group', 'head'), may hold values from 0 to 7
- state_cache: bfloat16 [32, 256, 64, 256], P('group', 'head'), may hold values from -16 to 16
Outputs:
- mixed: bfloat16 [4096, 8192], P('group', 'head')
- final_state: float32 [8, 256, 64, 256], P('group', 'head')
The draws below stay inside these ranges and needn't reach their ends.
Inputs may be any that keep to these rules, and one draw needn't show every extreme that they name: `hit_owner`: within the 2 x 8 block of one device (one index of group, one index of head), no owner is named by more than 6 entries, and one owner is named by exactly 6.
All inputs are finite; a program needn't handle non-finite values.
Results may differ from the reference program's by a relative error of at most 0.017.
Values may be sent and summed in bfloat16 or wider, within the bound.
A program may use at most 128 MiB of HBM per device.

```python
import jax
import jax.numpy as jnp
from jax import lax

D = 8192
P_SIZE = 64
N = 256
NG = 8
SPAN = 128
H_DEV = 8
LEN = 512
SESS = 2
SLOTS = 8
CAP = 6
HEADS = 256
D_INNER = 16384
SPANS = 4
SESSIONS = 8
TOKENS = 4096
CACHE_SLOTS = 32


def draw_hit_owner(key, part):
    key = jax.random.fold_in(key, 11)
    group_total = SESSIONS // SESS
    head_blocks = HEADS // H_DEV
    block_size = SESS * H_DEV
    block_total = group_total * head_blocks
    first_key, second_key, third_key = jax.random.split(key, 3)
    leading = jax.random.randint(first_key, (block_total, 1), 0, group_total)
    offsets = jax.random.randint(second_key, (block_total, 1), 0, group_total - 1)
    places = jnp.arange(block_size, dtype=jnp.int32)[None, :]
    others = (leading + 1 + (places - CAP + offsets) % (group_total - 1)) % group_total
    owners = jnp.where(places < CAP, leading, others).astype(jnp.int32)
    order_keys = jax.random.split(third_key, block_total)
    orders = jax.vmap(lambda single: jax.random.permutation(single, block_size))(order_keys)
    owners = jnp.take_along_axis(owners, orders, axis=1)
    owners = owners.reshape(group_total, head_blocks, SESS, H_DEV).transpose(0, 2, 1, 3)
    return owners.reshape(SESSIONS, HEADS).astype(jnp.int32)


def draw_decay_log(key, part):
    key = jax.random.fold_in(key, 23)
    values = jax.random.uniform(key, (HEADS,), jnp.float32, -6.2, -2.3)
    return values.astype(jnp.float32)


def draw_state_cache(key, part):
    key = jax.random.fold_in(key, 37)
    shape = (CACHE_SLOTS, HEADS, P_SIZE, N)
    values = jnp.clip(jax.random.normal(key, shape, jnp.float32), -4.0, 4.0) * 4.0
    return values.astype(jnp.bfloat16)


def with_ends(drawn, stream_key, low, top_value):
    longest = drawn.shape.index(max(drawn.shape))
    spots = []
    for shift in (0, 1):
        where = [jax.random.randint(jax.random.fold_in(stream_key, axis), (), 0, length) for axis, length in enumerate(drawn.shape)]
        where[longest] = (where[longest] + shift) % drawn.shape[longest]
        spots.append(tuple(where))
    return drawn.at[spots[0]].set(low).at[spots[1]].set(top_value)


def with_spikes(array, rng, source, target, parts, factor):
    def block_of(axis_at):
        return (jnp.arange(array.shape[axis_at]) // (array.shape[axis_at] // parts)).reshape((-1,) + (1,) * (array.ndim - 1 - axis_at))

    near = jax.random.permutation(rng, parts)[block_of(target)]
    far = (block_of(target) + parts // 2) % parts
    return jnp.where((block_of(source) == near) | (block_of(source) == far), factor * array, array)


def block_levels(rng, dims, pieces, smallest, high):
    def one(dim, parts):
        draws = jax.random.uniform(jax.random.fold_in(jax.random.fold_in(rng, 6), dim), (parts,), jnp.float32, smallest / len(pieces), high / len(pieces))
        return jnp.repeat(jnp.exp(draws), dims[dim] // parts).reshape((-1,) + (1,) * (len(dims) - dim - 1))

    gain = one(*pieces[0])
    for cut in pieces[1:]:
        gain = gain * one(*cut)
    return gain


def bell_draw(rng, extent, spread, limit, cuts=(), kind=jnp.bfloat16):
    loudness = block_levels(rng, extent, cuts, -0.22, 0.18) if cuts else 1.0
    array = jax.random.normal(rng, extent, jnp.float32) * spread * loudness
    return jnp.minimum(jnp.maximum(array, -limit), limit).astype(kind)


def bell_draw_with(rng, extent, width, reach, shards, heavy, kind=jnp.bfloat16):
    array = width * jax.random.normal(rng, extent, jnp.float32)
    if shards:
        array = array * block_levels(rng, extent, shards, -0.22, 0.18)
    return jnp.clip(with_spikes(array, jax.random.fold_in(rng, 3), *heavy), -reach, reach).astype(kind)


def setup_inputs(seed: int = 0) -> dict:
    arg_keys = jax.random.split(jax.random.key(seed), 15)
    mixer_input = bell_draw(arg_keys[0], (TOKENS, D_INNER), 1.0, 6.0, ((0, 4), (1, 32)))
    gate_input = bell_draw(arg_keys[1], (TOKENS, D_INNER), 1.0, 6.0, ((0, 4), (1, 32)))
    step_raw = bell_draw(arg_keys[2], (TOKENS, HEADS), 1.0, 5.0, ((0, 4), (1, 32)), jnp.float32)
    state_proj = bell_draw(arg_keys[3], (2, TOKENS, NG, N), 0.125, 0.75, ((1, 4),))
    decay_log = draw_decay_log(jax.random.fold_in(arg_keys[14], 71), 0)
    step_bias = jnp.clip(-2.0 + 2.5 * jax.random.uniform(arg_keys[5], (HEADS,), jnp.float32) ** block_levels(arg_keys[5], (HEADS,), ((0, 32),), -0.2, 0.2), -2.0, 0.5)
    skip_gain = jnp.clip(0.3 + 1.7 * jax.random.uniform(arg_keys[6], (HEADS,), jnp.float32) ** block_levels(arg_keys[6], (HEADS,), ((0, 32),), -0.2, 0.2), 0.3, 2.0)
    norm_gain = jnp.clip(1.0 + 0.1 * jax.random.normal(arg_keys[7], (D_INNER,), jnp.float32), 0.5, 1.5)
    out_weight = bell_draw_with(arg_keys[8], (D_INNER, D), D_INNER ** -0.5, 0.09375, ((0, 32),), (0, 1, 32, 2.75))
    residual = bell_draw(arg_keys[9], (TOKENS, D), 1.0, 6.0, ((0, 4), (1, 32)))
    new_spans = with_ends(jax.random.randint(arg_keys[10], (SESSIONS,), 1, SPANS + 1), jax.random.fold_in(arg_keys[10], 1), 1, SPANS).astype(jnp.int32)
    hit_owner = draw_hit_owner(jax.random.fold_in(arg_keys[14], 71), 0)
    hit_slot = with_ends(jax.random.randint(arg_keys[12], (SESSIONS, HEADS), 0, SLOTS), jax.random.fold_in(arg_keys[12], 1), 0, SLOTS - 1).astype(jnp.int32)
    state_cache = draw_state_cache(jax.random.fold_in(arg_keys[14], 71), 0)
    return {"mixer_input": mixer_input, "gate_input": gate_input, "step_raw": step_raw, "state_proj": state_proj, "decay_log": decay_log, "step_bias": step_bias, "skip_gain": skip_gain, "norm_gain": norm_gain, "out_weight": out_weight, "residual": residual, "new_spans": new_spans, "hit_owner": hit_owner, "hit_slot": hit_slot, "state_cache": state_cache}


def reference(mixer_input, gate_input, step_raw, state_proj, decay_log, step_bias, skip_gain, norm_gain, out_weight, residual, new_spans, hit_owner, hit_slot, state_cache):
    highest = lax.Precision.HIGHEST
    per_group = HEADS // NG
    live = (jnp.arange(LEN, dtype=jnp.int32)[None, :] < (new_spans * SPAN)[:, None]).astype(jnp.float32)
    steps = jax.nn.softplus(step_raw.reshape(SESSIONS, LEN, HEADS) + step_bias) * live[:, :, None]
    rates = -jnp.exp(decay_log) * steps
    shape_five = (SESSIONS, SPANS, SPAN, NG, per_group)
    steps = steps.reshape(shape_five)
    cumulative = jnp.cumsum(rates.reshape(shape_five), axis=2)
    values = mixer_input.astype(jnp.float32).reshape(SESSIONS, SPANS, SPAN, NG, per_group, P_SIZE)
    inputs_b = state_proj[0].astype(jnp.float32).reshape(SESSIONS, SPANS, SPAN, NG, N)
    outputs_c = state_proj[1].astype(jnp.float32).reshape(SESSIONS, SPANS, SPAN, NG, N)
    wanted = (hit_owner * SLOTS + hit_slot).astype(jnp.int32)
    head_ids = jnp.arange(HEADS, dtype=jnp.int32)[None, :]
    start_state = state_cache[wanted, head_ids].astype(jnp.float32).reshape(SESSIONS, NG, per_group, P_SIZE, N)
    lower = jnp.arange(SPAN)[:, None] >= jnp.arange(SPAN)[None, :]

    def span_step(carried, inputs):
        values_c, inputs_c, reads_c, steps_c, cumul_c = inputs
        scores = jnp.einsum('stgn,sugn->stug', reads_c, inputs_c, precision=highest)
        differ = cumul_c[:, :, None] - cumul_c[:, None, :]
        weights = jnp.where(lower[None, :, :, None, None], jnp.exp(jnp.minimum(differ, 0.0)), 0.0)
        weights = weights * scores[..., None] * steps_c[:, None]
        weights = lax.optimization_barrier(weights.astype(jnp.bfloat16)).astype(jnp.float32)
        within = jnp.einsum('stugi,sugip->stgip', weights, values_c, precision=highest)
        carried_in = jnp.einsum('stgn,sgipn->stgip', reads_c, carried, precision=highest) * jnp.exp(cumul_c)[..., None]
        to_end = jnp.exp(cumul_c[:, -1:] - cumul_c) * steps_c
        scaled = lax.optimization_barrier((to_end[..., None] * values_c).astype(jnp.bfloat16)).astype(jnp.float32)
        update = jnp.einsum('sugip,sugn->sgipn', scaled, inputs_c, precision=highest)
        carried_next = jnp.exp(cumul_c[:, -1])[..., None, None] * carried + update
        result = within + carried_in + skip_gain.reshape(NG, per_group)[None, None, :, :, None] * values_c
        return (carried_next, result)
    scanned = tuple((jnp.moveaxis(member, 1, 0) for member in (values, inputs_b, outputs_c, steps, cumulative)))
    carried_final, outputs = lax.scan(span_step, start_state, scanned)
    outputs = jnp.moveaxis(outputs, 0, 1).reshape(TOKENS, D_INNER)
    gated = outputs * jax.nn.silu(gate_input.astype(jnp.float32))
    mean_square = lax.optimization_barrier(jnp.mean(gated * gated, axis=1, keepdims=True))
    normed = (gated * lax.rsqrt(mean_square + 1e-05) * norm_gain).astype(jnp.bfloat16)
    block_width = H_DEV * P_SIZE

    def add_block(index, total):
        columns = lax.dynamic_slice_in_dim(normed, index * block_width, block_width, 1)
        rows_w = lax.dynamic_slice_in_dim(out_weight, index * block_width, block_width, 0)
        term = jnp.dot(columns, rows_w, preferred_element_type=jnp.float32)
        return total + lax.optimization_barrier(term.astype(jnp.bfloat16)).astype(jnp.float32)
    summed = lax.fori_loop(0, HEADS // H_DEV, add_block, jnp.zeros((TOKENS, D), jnp.float32))
    mixed = (residual.astype(jnp.float32) + summed).astype(jnp.bfloat16)
    final_state = carried_final.reshape(SESSIONS, HEADS, P_SIZE, N)
    return (mixed, final_state)
```

```python
import jax
import jax.numpy as jnp
from jax import lax
from jax.experimental import pallas as pl
from jax.experimental.pallas import tpu as pltpu
from jax.sharding import PartitionSpec as P

SPAN = 128

HALF = (0, 1)
ORDER = ((2, 0), (2, 1), (0, 2), (1, 2), (2, 2), (2, 3), (3, 2), (1, 3), (3, 0), (3, 1), (0, 3), (1, 0), (1, 1), (3, 3), (0, 1), (0, 0))
SIDE = 4
CHUNKS = 4
MESH = pl.DeviceIdType.MESH
BF16 = jnp.bfloat16
F32 = jnp.float32


def remote(src, dst, send_sem, recv_sem, head):
    return pltpu.make_async_remote_copy(
        src_ref=src, dst_ref=dst, send_sem=send_sem, recv_sem=recv_sem,
        device_id={"head": head}, device_id_type=MESH,
    )


def project_kernel(
    w_hbm, g_own, ss_in, res, out,
    w_own, w_part, g_part, s1, own1, r1o, r1n, s2, acc, r2o, r2n,
    ss_mid, ss_core, ss_x, ss_y,
    sem_w, sem_ws, sem_wr, sem_gs, sem_gr, sem_1s, sem_1r, sem_2s, sem_2r, sem_ss, sem_sr,
):
    me = lax.axis_index("head")
    core = lax.rem(me, 2)
    col = lax.rem(me // 2, SIDE)
    row = me // (2 * SIDE)

    def head_at(dx, dy, dc):
        y = lax.rem(row + dy, SIDE)
        x = lax.rem(col + dx, SIDE)
        c = lax.rem(core + dc, 2)
        return (y * SIDE + x) * 2 + c

    partner = head_at(0, 0, 1)
    x_peers = [head_at(k, 0, 0) for k in (1, 2, 3)]
    y_peers = [head_at(0, k, 0) for k in (1, 2, 3)]
    p_side = ((x_peers[0], x_peers[2]), (y_peers[0], y_peers[2]))
    q_side = (p_side[1], p_side[0])

    barrier = pltpu.get_barrier_semaphore()
    for peer in [partner] + x_peers + y_peers:
        pl.semaphore_signal(barrier, inc=1, device_id={"head": peer}, device_id_type=MESH)

    def w_local(i, dx, dy):
        start = pl.multiple_of(head_at(dx, dy, 0) * 256, 256)
        return pltpu.make_async_copy(w_hbm.at[:, pl.ds(start, 256)], w_own.at[dx, dy], sem_w.at[i])

    def w_remote(i, dx, dy):
        start = pl.multiple_of(head_at(dx, dy, 1) * 256, 256)
        return remote(w_hbm.at[:, pl.ds(start, 256)], w_part.at[dx, dy], sem_ws.at[i], sem_wr.at[i], partner)

    def g_remote(c):
        return remote(g_own.at[c], g_part.at[c], sem_gs.at[c], sem_gr.at[c], partner)

    for i, (dx, dy) in enumerate(ORDER):
        w_local(i, dx, dy).start()
    pl.semaphore_wait(barrier, 7)
    g_remote(0).start()
    for i, (dx, dy) in enumerate(ORDER):
        w_remote(i, dx, dy).start()
    for c in range(1, CHUNKS):
        g_remote(c).start()

    def ss_core_copy():
        return remote(ss_in, ss_core, sem_ss.at[0], sem_sr.at[0], partner)

    def ss_x_copy(k):
        return remote(ss_mid.at[0], ss_x.at[k], sem_ss.at[1 + k], sem_sr.at[1 + k], x_peers[k])

    def ss_y_copy(k):
        return remote(ss_mid.at[1], ss_y.at[k], sem_ss.at[4 + k], sem_sr.at[4 + k], y_peers[k])

    ss_core_copy().start()

    def first(part, c, kind):
        if kind == 0:
            src, dst, way = s1.at[part, c, 1, 0], r1o.at[part, c, 0], 0
        elif kind == 1:
            src, dst, way = s1.at[part, c, 1, 1], r1o.at[part, c, 1], 1
        elif kind == 2:
            src, dst, way = s1.at[part, c, 0, 1], r1n.at[part, c, 0, 1], 0
        elif kind == 3:
            src, dst, way = s1.at[part, c, 2, 0], r1n.at[part, c, 1, 0], 1
        elif kind == 4:
            src, dst, way = s1.at[part, c, 0, 0], r1n.at[part, c, 0, 0], 0
        else:
            src, dst, way = s1.at[part, c, 2, 1], r1n.at[part, c, 1, 1], 1
        return remote(src, dst, sem_1s.at[part, c, kind], sem_1r.at[part, c, kind], p_side[part][way])

    def second(part, c, kind):
        if kind == 0:
            src, dst, way = s2.at[part, c, 1, 0], r2o.at[part, c, 0], 0
        elif kind == 1:
            src, dst, way = s2.at[part, c, 1, 1], r2o.at[part, c, 1], 1
        elif kind == 2:
            src, dst, way = s2.at[part, c, 0, 1], r2n.at[part, c, 0, 1], 0
        elif kind == 3:
            src, dst, way = s2.at[part, c, 2, 0], r2n.at[part, c, 1, 0], 1
        elif kind == 4:
            src, dst, way = s2.at[part, c, 0, 0], r2n.at[part, c, 0, 0], 0
        else:
            src, dst, way = s2.at[part, c, 2, 1], r2n.at[part, c, 1, 1], 1
        return remote(src, dst, sem_2s.at[part, c, kind], sem_2r.at[part, c, kind], q_side[part][way])

    IMMEDIATE = {(2, 0): 0, (2, 1): 1, (1, 1): 2, (3, 0): 3}

    def stage_project(c):
        g_remote(c).wait_recv()
        done = set()
        for i, (dx, dy) in enumerate(ORDER):
            @pl.when(c == 0)
            def _():
                w_local(i, dx, dy).wait()
                w_remote(i, dx, dy).wait_recv()
            term = jnp.dot(g_own[c], w_own[dx, dy], preferred_element_type=F32)
            term += jnp.dot(g_part[c], w_part[dx, dy], preferred_element_type=F32)
            for part, dp, dq in ((0, dx, dy), (1, dy, dx)):
                piece = term[part * SPAN:(part + 1) * SPAN]
                columns = pl.ds((dq % 2) * 256, 256)
                if dp == 0:
                    own1[part, c, dq // 2, :, columns] = piece
                else:
                    s1[part, c, dp - 1, dq // 2, :, columns] = piece.astype(BF16)
                done.add((part, dp, dq))
                pair = (part, dp, dq - dq % 2), (part, dp, dq - dq % 2 + 1)
                kind = IMMEDIATE.get((dp, dq // 2))
                if kind is not None and pair[0] in done and pair[1] in done:
                    first(part, c, kind).start()

    def stage_pass1(c):
        for part in (0, 1):
            for way, (dp, half) in enumerate(((0, 0), (2, 1))):
                first(part, c, way).wait_recv()
                total = s1[part, c, dp, half].astype(F32) + r1o[part, c, way].astype(F32)
                s1[part, c, dp, half] = total.astype(BF16)
                first(part, c, 4 + way).start()

    def stage_turn(c):
        for part in (0, 1):
            sums = [None, None]
            for half in (1, 0):
                first(part, c, 2 if half else 4).wait_recv()
                first(part, c, 5 if half else 3).wait_recv()
                sums[half] = own1[part, c, half] + r1n[part, c, 0, half].astype(F32) + r1n[part, c, 1, half].astype(F32)
                if half:
                    s2[part, c, 1, 0] = sums[1][:64, :256].astype(BF16)
                    second(part, c, 0).start()
                    s2[part, c, 1, 1] = sums[1][64:, :256].astype(BF16)
                    second(part, c, 1).start()
                    s2[part, c, 2, 0] = sums[1][:64, 256:].astype(BF16)
                    second(part, c, 3).start()
                    s2[part, c, 2, 1] = sums[1][64:, 256:].astype(BF16)
                else:
                    s2[part, c, 0, 1] = sums[0][64:, 256:].astype(BF16)
                    second(part, c, 2).start()
                    s2[part, c, 0, 0] = sums[0][:64, 256:].astype(BF16)
                    acc[part, c] = sums[0][:, :256]

    def stage_pass2(c):
        for part in (0, 1):
            for way, (dp, half) in enumerate(((0, 0), (2, 1))):
                second(part, c, way).wait_recv()
                total = s2[part, c, dp, half].astype(F32) + r2o[part, c, way].astype(F32)
                s2[part, c, dp, half] = total.astype(BF16)
                second(part, c, 4 + way).start()

    def stage_last(c):
        for part in (0, 1):
            for half in (0, 1):
                second(part, c, 2 if half else 4).wait_recv()
                second(part, c, 5 if half else 3).wait_recv()
                acc[part, c, pl.ds(half * 64, 64)] += (
                    r2n[part, c, 0, half].astype(F32) + r2n[part, c, 1, half].astype(F32)
                )

    def step(t, _):
        @pl.when(t < CHUNKS)
        def _():
            stage_project(t)

        @pl.when(t == 0)
        def _():
            ss_core_copy().wait()
            ss_mid[0] = ss_in[...] + ss_core[...]
            for k in range(3):
                ss_x_copy(k).start()

        @pl.when(t == 1)
        def _():
            for k in range(3):
                ss_x_copy(k).wait()
            ss_mid[1] = ss_mid[0] + ss_x[0] + ss_x[1] + ss_x[2]
            for k in range(3):
                ss_y_copy(k).start()

        for lag, stage in ((1, stage_pass1), (2, stage_turn), (3, stage_pass2), (4, stage_last)):
            @pl.when(jnp.logical_and(t >= lag, t < CHUNKS + lag))
            def _():
                stage(t - lag)
        return 0

    lax.fori_loop(0, CHUNKS + 4, step, 0)

    for k in range(3):
        ss_y_copy(k).wait()
    total = ss_mid[1] + ss_y[0] + ss_y[1] + ss_y[2]
    scale = lax.rsqrt(total / 16384.0 + 1e-05)
    scale = jnp.transpose(jnp.concatenate([scale] * 16, axis=0))
    for part in (0, 1):
        for c in range(CHUNKS):
            block = part * CHUNKS + c
            rows = pl.ds(block * SPAN, SPAN)
            out[rows, :] = (
                res[rows, :].astype(F32) + acc[part, c] * scale[:, block:block + 1]
            ).astype(BF16)

    def drain(c, _):
        for part in (0, 1):
            for kind in range(6):
                first(part, c, kind).wait_send()
                second(part, c, kind).wait_send()
        g_remote(c).wait_send()
        return 0

    lax.fori_loop(0, CHUNKS, drain, 0)
    for i, (dx, dy) in enumerate(ORDER):
        w_remote(i, dx, dy).wait_send()


def project(w, g, ss, res):
    vmem = pl.BlockSpec(memory_space=pltpu.VMEM)
    dma = pltpu.SemaphoreType.DMA
    return pl.pallas_call(
        project_kernel,
        out_shape=jax.ShapeDtypeStruct(res.shape, res.dtype),
        in_specs=[pl.BlockSpec(memory_space=pl.ANY), vmem, vmem, vmem],
        out_specs=vmem,
        scratch_shapes=[
            pltpu.VMEM((4, 4, 512, 256), BF16),
            pltpu.VMEM((4, 4, 512, 256), BF16),
            pltpu.VMEM((4, 256, 512), BF16),
            pltpu.VMEM((2, 4, 3, 2, 128, 512), BF16),
            pltpu.VMEM((2, 4, 2, 128, 512), F32),
            pltpu.VMEM((2, 4, 2, 128, 512), BF16),
            pltpu.VMEM((2, 4, 2, 2, 128, 512), BF16),
            pltpu.VMEM((2, 4, 3, 2, 64, 256), BF16),
            pltpu.VMEM((2, 4, 128, 256), F32),
            pltpu.VMEM((2, 4, 2, 64, 256), BF16),
            pltpu.VMEM((2, 4, 2, 2, 64, 256), BF16),
            pltpu.VMEM((2, 8, 128), F32),
            pltpu.VMEM((8, 128), F32),
            pltpu.VMEM((3, 8, 128), F32),
            pltpu.VMEM((3, 8, 128), F32),
            dma((16,)), dma((16,)), dma((16,)), dma((4,)), dma((4,)),
            dma((2, 4, 6)), dma((2, 4, 6)), dma((2, 4, 6)), dma((2, 4, 6)),
            dma((7,)), dma((7,)),
        ],
        compiler_params=pltpu.CompilerParams(
            collective_id=0, has_side_effects=True, vmem_limit_bytes=50 * 1024 * 1024
        ),
        cost_estimate=pl.CostEstimate(flops=8600000000, bytes_accessed=12000000, transcendentals=0),
        name="project",
    )(w, g, ss, res)


def per_device(
    mixer_input,
    gate_input,
    step_raw,
    state_proj,
    decay_log,
    step_bias,
    skip_gain,
    norm_gain,
    out_weight,
    residual,
    new_spans,
    hit_owner,
    hit_slot,
    state_cache,
):
    highest = lax.Precision.HIGHEST
    session_count = new_spans.shape[0]
    head_count = decay_log.shape[0]
    row_count = mixer_input.shape[0]
    turn_length = row_count // session_count
    span_count = turn_length // SPAN
    head_width = mixer_input.shape[1] // head_count
    state_width = state_proj.shape[3]
    group_count = state_proj.shape[2]
    per_group = head_count * lax.axis_size("head") // group_count
    group_index = lax.axis_index("head") * head_count // per_group
    block_count = session_count * head_count
    owners = hit_owner.reshape(block_count)
    slot_index = hit_slot.reshape(block_count)
    local_head = jnp.arange(block_count, dtype=jnp.int32) % head_count
    flat_width = head_width * state_width
    every_cache = lax.all_gather(state_cache, "group", axis=0, tiled=True)
    slot_count = state_cache.shape[0]
    flat_cache = every_cache.reshape(-1, flat_width)
    wanted = (owners * slot_count + slot_index) * head_count + local_head
    fetched = jnp.take(flat_cache, wanted, axis=0)
    start_state = fetched.astype(jnp.float32).reshape(
        session_count, head_count, head_width, state_width
    )
    live = (jnp.arange(turn_length, dtype=jnp.int32)[None, :] < (new_spans * SPAN)[:, None]).astype(
        jnp.float32
    )
    steps = (
        jax.nn.softplus(step_raw.reshape(session_count, turn_length, head_count) + step_bias)
        * live[:, :, None]
    )
    rates = -jnp.exp(decay_log) * steps
    shape_four = (session_count, span_count, SPAN, head_count)
    steps = steps.reshape(shape_four)
    cumulative = jnp.cumsum(rates.reshape(shape_four), axis=2)
    values = mixer_input.reshape(session_count, span_count, SPAN, head_count, head_width)
    inputs_b = lax.dynamic_index_in_dim(state_proj[0], group_index, 1, keepdims=False)
    inputs_b = inputs_b.reshape(session_count, span_count, SPAN, state_width)
    outputs_c = lax.dynamic_index_in_dim(state_proj[1], group_index, 1, keepdims=False)
    outputs_c = outputs_c.reshape(session_count, span_count, SPAN, state_width)
    lower = jnp.arange(SPAN)[:, None] >= jnp.arange(SPAN)[None, :]

    def span_step(carried, inputs):
        values_c, inputs_c, reads_c, steps_c, cumul_c = inputs
        scores = jnp.einsum("stn,sun->stu", reads_c, inputs_c, preferred_element_type=jnp.float32)
        differ = cumul_c[:, :, None] - cumul_c[:, None, :]
        weights = jnp.where(lower[None, :, :, None], jnp.exp(jnp.minimum(differ, 0.0)), 0.0)
        weights = (weights * scores[..., None] * steps_c[:, None]).astype(jnp.bfloat16)
        within = jnp.einsum(
            "stuh,suhp->sthp", weights, values_c, preferred_element_type=jnp.float32
        )
        carried_in = (
            jnp.einsum("stn,shpn->sthp", reads_c.astype(jnp.float32), carried, precision=highest)
            * jnp.exp(cumul_c)[..., None]
        )
        to_end = jnp.exp(cumul_c[:, -1:] - cumul_c) * steps_c
        scaled = (to_end[..., None] * values_c.astype(jnp.float32)).astype(jnp.bfloat16)
        update = jnp.einsum("suhp,sun->shpn", scaled, inputs_c, preferred_element_type=jnp.float32)
        carried_next = jnp.exp(cumul_c[:, -1])[..., None, None] * carried + update
        result = within + carried_in + skip_gain[None, None, :, None] * values_c.astype(jnp.float32)
        return (carried_next, result)

    scanned = tuple(
        (jnp.moveaxis(member, 1, 0) for member in (values, inputs_b, outputs_c, steps, cumulative))
    )
    carried_final, outputs = lax.scan(span_step, start_state, scanned)
    outputs = jnp.moveaxis(outputs, 0, 1).reshape(row_count, head_count * head_width)
    gated = outputs * jax.nn.silu(gate_input.astype(jnp.float32))
    ss = jnp.sum(gated * gated, axis=1).reshape(8, 128)
    scaled_out = (gated * norm_gain).astype(jnp.bfloat16)
    scaled_out = jnp.moveaxis(scaled_out.reshape(2, 4, 128, 512), 0, 1).reshape(4, 256, 512)
    mixed = project(out_weight, scaled_out, ss, residual)
    return (mixed, carried_final)


def solution(mesh):
    in_specs = (
        P("group", "head"),
        P("group", "head"),
        P("group", "head"),
        P(None, "group", None, None),
        P("head"),
        P("head"),
        P("head"),
        P("head"),
        P("head", None),
        P("group", "head"),
        P("group"),
        P("group", "head"),
        P("group", "head"),
        P("group", "head", None, None),
    )
    out_specs = (P("group", "head"), P("group", "head", None, None))
    return jax.shard_map(
        per_device, mesh=mesh, in_specs=in_specs, out_specs=out_specs, check_vma=False
    )
```

```python
import jax
import jax.numpy as jnp
from jax import lax
from jax.experimental import pallas as pl
from jax.experimental.pallas import tpu as pltpu
from jax.sharding import PartitionSpec as P

SPAN = 128
CAP = 6
ORDER = (
    (2, 0), (2, 1), (0, 2), (1, 2), (2, 2), (2, 3), (3, 2), (1, 3),
    (3, 0), (3, 1), (0, 3), (1, 0), (1, 1), (3, 3), (0, 1), (0, 0),
)
SIDE = 4
CHUNKS = 4
BLOCKS = 8
MESH = pl.DeviceIdType.MESH
BF16 = jnp.bfloat16
F32 = jnp.float32
I32 = jnp.int32
HIGHEST = lax.Precision.HIGHEST


def remote(src, dst, send_sem, recv_sem, where):
    return pltpu.make_async_remote_copy(
        src_ref=src, dst_ref=dst, send_sem=send_sem, recv_sem=recv_sem,
        device_id=where, device_id_type=MESH,
    )


def dot_tn(a, b):
    return lax.dot_general(a, b, (((0,), (0,)), ((), ())), preferred_element_type=F32)


def dot_nt(a, b):
    return lax.dot_general(a, b, (((1,), (1,)), ((), ())), preferred_element_type=F32)


def mixer_kernel(
    owner_s, slot_s, spans_s, decay_s, bias_s, skip_s,
    x_hbm, gate_hbm, step_hbm, sp_hbm, gain_hbm, w_hbm, res_hbm, cache_hbm,
    out, state_out,
    x_v, gate_v, step_v, sp_v, gain_v, res, cache_v,
    req_v, rreq, req_s, idx_s, pbuf, rbuf, relay,
    e_v, f_v, em_v, sel_v, yi_v, ee_v, u_v, c_v, h_v, hb_v, ssa, ss_in,
    w_own, w_part, g_own, g_part, s1, own1, r1o, r1n, s2, acc, r2o, r2n,
    ss_mid, ss_core, ss_x, ss_y,
    sem_in, sem_sp, sem_req_s, sem_req_r, sem_rs, sem_st_s, sem_st_r, sem_out,
    sem_w, sem_ws, sem_wr, sem_gs, sem_gr, sem_1s, sem_1r, sem_2s, sem_2r, sem_ss, sem_sr,
):
    me = lax.axis_index("head")
    deep = lax.axis_index("group")
    core = lax.rem(me, 2)
    col = lax.rem(me // 2, SIDE)
    row = me // (2 * SIDE)

    def head_at(dx, dy, dc):
        y = lax.rem(row + dy, SIDE)
        x = lax.rem(col + dx, SIDE)
        c = lax.rem(core + dc, 2)
        return (y * SIDE + x) * 2 + c

    def at_head(h):
        return {"head": h}

    partner = at_head(head_at(0, 0, 1))
    x_peers = [at_head(head_at(k, 0, 0)) for k in (1, 2, 3)]
    y_peers = [at_head(head_at(0, k, 0)) for k in (1, 2, 3)]
    z_peers = [{"group": lax.rem(deep + k, 4)} for k in (1, 2, 3)]
    p_side = ((x_peers[0], x_peers[2]), (y_peers[0], y_peers[2]))
    q_side = (p_side[1], p_side[0])

    barrier = pltpu.get_barrier_semaphore()
    for peer in z_peers + [partner] + x_peers + y_peers:
        pl.semaphore_signal(barrier, inc=1, device_id=peer, device_id_type=MESH)

    loads = [
        pltpu.make_async_copy(src, dst, sem_in.at[i])
        for i, (src, dst) in enumerate((
            (cache_hbm, cache_v), (step_hbm, step_v), (x_hbm, x_v), (gain_hbm, gain_v),
            (gate_hbm, gate_v), (res_hbm, res),
        ))
    ]

    def sp_copy(b):
        start = pl.multiple_of(b * 1024, 1024)
        return pltpu.make_async_copy(sp_hbm.at[:, pl.ds(start, 1024)], sp_v.at[b], sem_sp.at[b])

    def w_local(i, dx, dy):
        start = pl.multiple_of(head_at(dx, dy, 0) * 256, 256)
        return pltpu.make_async_copy(w_hbm.at[:, pl.ds(start, 256)], w_own.at[dx, dy], sem_w.at[i])

    def w_remote(i, dx, dy):
        start = pl.multiple_of(head_at(dx, dy, 1) * 256, 256)
        return remote(w_hbm.at[:, pl.ds(start, 256)], w_part.at[dx, dy], sem_ws.at[i], sem_wr.at[i], partner)

    def g_remote(c):
        return remote(g_own.at[c], g_part.at[c], sem_gs.at[c], sem_gr.at[c], partner)

    for load in loads[:5]:
        load.start()
    for b in range(BLOCKS):
        sp_copy(b).start()

    lane = lax.broadcasted_iota(I32, (8, 128), 1)
    request = jnp.zeros((8, 128), I32)
    seen = jnp.zeros((8, 128), I32)
    counts = [jnp.int32(0)] * 4
    for e in range(16):
        s, j = divmod(e, 8)
        owner = owner_s[s, j]
        place = slot_s[s, j] * 8 + j
        named = (lane // 8) == owner
        request = jnp.where(jnp.logical_and(named, seen == lane % 8), place, request)
        seen = seen + jnp.where(named, 1, 0)
        rank = jnp.int32(0)
        for q in range(4):
            rank = jnp.where(owner == q, counts[q], rank)
            counts[q] = counts[q] + jnp.where(owner == q, 1, 0)
        away = lax.rem(owner - deep + 4, 4)
        idx_s[0, e] = jnp.where(away == 0, 0, (away - 1) * CAP + jnp.minimum(rank, CAP - 1))
        idx_s[1, e] = jnp.where(away == 0, 1, 0)
        idx_s[2, e] = place
    req_v[...] = request

    def req_copy(k):
        return remote(req_v, rreq.at[k], sem_req_s.at[k], sem_req_r.at[k], z_peers[k])

    pl.semaphore_wait(barrier, 10)
    for k in (1, 0, 2):
        req_copy(k).start()
    for i, (dx, dy) in enumerate(ORDER):
        w_local(i, dx, dy).start()
    for i, (dx, dy) in enumerate(ORDER):
        w_remote(i, dx, dy).start()
    loads[5].start()

    sub = lax.broadcasted_iota(I32, (8, 128), 0)
    bias = jnp.zeros((8, 128), F32)
    decay = jnp.zeros((8, 128), F32)
    for j in range(8):
        bias = jnp.where(sub == j, bias_s[j], bias)
        decay = jnp.where(sub == j, decay_s[j], decay)
    decay = -jnp.exp(decay)
    loads[1].wait()
    steps = []
    for b in range(BLOCKS):
        raw = step_v[:, b * SPAN:(b + 1) * SPAN] + bias
        alive = jnp.where(b % CHUNKS < spans_s[b // CHUNKS], 1.0, 0.0)
        steps.append((jnp.maximum(raw, 0.0) + jnp.log1p(jnp.exp(-jnp.abs(raw)))) * alive)
    dt = jnp.concatenate(steps, axis=0)
    rate = jnp.concatenate([decay * step for step in steps], axis=0)
    square0 = lax.broadcasted_iota(I32, (SPAN, SPAN), 0)
    square1 = lax.broadcasted_iota(I32, (SPAN, SPAN), 1)
    upper = jnp.where(square0 <= square1, 1.0, 0.0).astype(F32)
    cum = jnp.dot(rate, upper, precision=HIGHEST, preferred_element_type=F32)
    middle = cum[:, SPAN - 1:] * 0.5
    e_v[...] = jnp.exp(cum - middle)
    f_v[...] = jnp.exp(middle - cum) * dt
    em_v[...] = jnp.exp(jnp.broadcast_to(middle, (BLOCKS * 8, 128)))
    ssa[...] = jnp.zeros((SPAN, SPAN), F32)

    def rank_copy(k):
        return pltpu.make_async_copy(rreq.at[k], req_s.at[k], sem_rs.at[k])

    def state_copy(i):
        src, dst, way = (
            (pbuf.at[pl.ds(6, 3)], relay.at[0], 0),
            (pbuf.at[pl.ds(9, 3)], relay.at[1], 2),
            (pbuf.at[pl.ds(0, 6)], rbuf.at[pl.ds(0, 6)], 2),
            (pbuf.at[pl.ds(12, 6)], rbuf.at[pl.ds(12, 6)], 0),
            (relay.at[0], rbuf.at[pl.ds(6, 3)], 0),
            (relay.at[1], rbuf.at[pl.ds(9, 3)], 2),
        )[i]
        return remote(src, dst, sem_st_s.at[i], sem_st_r.at[i], z_peers[way])

    loads[0].wait()
    for k in (1, 0, 2):
        req_copy(k).wait_recv()
        rank_copy(k).start()
    for k in (1, 0, 2):
        rank_copy(k).wait()
        for r in range(CAP):
            pbuf[k * CAP + r] = cache_v[req_s[k, 0, deep * 8 + r]]
            if k == 1 and r == 2:
                state_copy(0).start()
        state_copy((2, 1, 3)[k]).start()

    pick = me // 4
    sel_v[...] = jnp.where(
        lax.broadcasted_iota(I32, (SPAN, 1024), 1) == lax.broadcasted_iota(I32, (SPAN, 1024), 0) * 8 + pick, 1.0, 0.0
    ).astype(BF16)
    channel = lax.broadcasted_iota(I32, (16, 512), 1)
    spread = jnp.where(channel // 64 == lax.broadcasted_iota(I32, (16, 512), 0) % 8, 1.0, 0.0).astype(BF16)
    channel = lax.broadcasted_iota(I32, (1, 512), 1)
    skip = jnp.zeros((1, 512), F32)
    for j in range(8):
        skip = jnp.where(channel // 64 == j, skip_s[j], skip)
    for load in loads[2:5]:
        load.wait()

    def widen(part):
        high = part.astype(BF16)
        low = (part - high.astype(F32)).astype(BF16)
        return dot_tn(jnp.concatenate([high, low], axis=0), spread)

    def prepare(b, _):
        sp_copy(b).wait()
        few = pl.ds(pl.multiple_of(b * 8, 8), 8)
        x = x_v[pl.ds(pl.multiple_of(b * SPAN, SPAN), SPAN), :].astype(F32)
        wide_e = widen(e_v[few, :])
        ee_v[b] = wide_e
        z = (widen(f_v[few, :]) * x).astype(BF16)
        b_rows = jnp.dot(sel_v[...], sp_v[b, 0], preferred_element_type=F32).astype(BF16)
        c_rows = jnp.dot(sel_v[...], sp_v[b, 1], preferred_element_type=F32).astype(BF16)
        c_v[b] = c_rows
        scores = jnp.where(square0 >= square1, dot_nt(c_rows, b_rows), 0.0).astype(BF16)
        yi_v[b] = wide_e * jnp.dot(scores, z, preferred_element_type=F32) + skip * x
        u_v[b] = dot_tn(z, b_rows)

        @pl.when(b == 2)
        def _():
            for i in (0, 1):
                state_copy(i).wait_recv()
                state_copy(4 + i).start()
        return 0

    lax.fori_loop(0, BLOCKS, prepare, 0)

    for i in (2, 3, 4, 5):
        state_copy(i).wait_recv()
    for e in range(16):
        s, j = divmod(e, 8)
        here = cache_v[idx_s[2, e]].astype(F32)
        sent = rbuf[idx_s[0, e]].astype(F32)
        h_v[s, j * 64:(j + 1) * 64, :] = jnp.where(idx_s[1, e] == 1, here, sent)

    def stage_states(c):
        for s in (0, 1):
            b = s * CHUNKS + c
            for j in range(8):
                rows = slice(j * 64, (j + 1) * 64)
                fade = em_v[pl.ds(b * 8 + j, 1), :]
                fade = jnp.concatenate([fade, fade], axis=1)
                faded = h_v[s, rows, :] * fade
                hb_v[s, rows, :] = faded.astype(BF16)
                h_v[s, rows, :] = (faded + u_v[b, rows, :]) * fade
            y = yi_v[b] + ee_v[b] * dot_nt(c_v[b], hb_v[s])
            gate = gate_v[pl.ds(pl.multiple_of(b * SPAN, SPAN), SPAN), :].astype(F32)
            gated = y * (gate / (1.0 + jnp.exp(-gate)))
            ssa[...] = jnp.where(square1 == b, jnp.sum(gated * gated, axis=1, keepdims=True), ssa[...])
            g_own[c, s * SPAN:(s + 1) * SPAN, :] = (gated * gain_v[...]).astype(BF16)
        g_remote(c).start()

    final_copy = pltpu.make_async_copy(h_v, state_out, sem_out)

    def ss_core_copy():
        return remote(ss_in, ss_core, sem_ss.at[0], sem_sr.at[0], partner)

    def ss_x_copy(k):
        return remote(ss_mid.at[0], ss_x.at[k], sem_ss.at[1 + k], sem_sr.at[1 + k], x_peers[k])

    def ss_y_copy(k):
        return remote(ss_mid.at[1], ss_y.at[k], sem_ss.at[4 + k], sem_sr.at[4 + k], y_peers[k])

    def first(part, c, kind):
        if kind == 0:
            src, dst, way = s1.at[part, c, 1, 0], r1o.at[part, c, 0], 0
        elif kind == 1:
            src, dst, way = s1.at[part, c, 1, 1], r1o.at[part, c, 1], 1
        elif kind == 2:
            src, dst, way = s1.at[part, c, 0, 1], r1n.at[part, c, 0, 1], 0
        elif kind == 3:
            src, dst, way = s1.at[part, c, 2, 0], r1n.at[part, c, 1, 0], 1
        elif kind == 4:
            src, dst, way = s1.at[part, c, 0, 0], r1n.at[part, c, 0, 0], 0
        else:
            src, dst, way = s1.at[part, c, 2, 1], r1n.at[part, c, 1, 1], 1
        return remote(src, dst, sem_1s.at[part, c, kind], sem_1r.at[part, c, kind], p_side[part][way])

    def second(part, c, kind):
        if kind == 0:
            src, dst, way = s2.at[part, c, 1, 0], r2o.at[part, c, 0], 0
        elif kind == 1:
            src, dst, way = s2.at[part, c, 1, 1], r2o.at[part, c, 1], 1
        elif kind == 2:
            src, dst, way = s2.at[part, c, 0, 1], r2n.at[part, c, 0, 1], 0
        elif kind == 3:
            src, dst, way = s2.at[part, c, 2, 0], r2n.at[part, c, 1, 0], 1
        elif kind == 4:
            src, dst, way = s2.at[part, c, 0, 0], r2n.at[part, c, 0, 0], 0
        else:
            src, dst, way = s2.at[part, c, 2, 1], r2n.at[part, c, 1, 1], 1
        return remote(src, dst, sem_2s.at[part, c, kind], sem_2r.at[part, c, kind], q_side[part][way])

    IMMEDIATE = {(2, 0): 0, (2, 1): 1, (1, 1): 2, (3, 0): 3}

    def stage_project(c):
        g_remote(c).wait_recv()
        done = set()
        for i, (dx, dy) in enumerate(ORDER):
            @pl.when(c == 0)
            def _():
                w_local(i, dx, dy).wait()
                w_remote(i, dx, dy).wait_recv()
            term = jnp.dot(g_own[c], w_own[dx, dy], preferred_element_type=F32)
            term += jnp.dot(g_part[c], w_part[dx, dy], preferred_element_type=F32)
            for part, dp, dq in ((0, dx, dy), (1, dy, dx)):
                piece = term[part * SPAN:(part + 1) * SPAN]
                columns = pl.ds((dq % 2) * 256, 256)
                if dp == 0:
                    own1[part, c, dq // 2, :, columns] = piece
                else:
                    s1[part, c, dp - 1, dq // 2, :, columns] = piece.astype(BF16)
                done.add((part, dp, dq))
                pair = (part, dp, dq - dq % 2), (part, dp, dq - dq % 2 + 1)
                kind = IMMEDIATE.get((dp, dq // 2))
                if kind is not None and pair[0] in done and pair[1] in done:
                    first(part, c, kind).start()

    def stage_pass1(c):
        for part in (0, 1):
            for way, (dp, half) in enumerate(((0, 0), (2, 1))):
                first(part, c, way).wait_recv()
                total = s1[part, c, dp, half].astype(F32) + r1o[part, c, way].astype(F32)
                s1[part, c, dp, half] = total.astype(BF16)
                first(part, c, 4 + way).start()

    def stage_turn(c):
        for part in (0, 1):
            sums = [None, None]
            for half in (1, 0):
                first(part, c, 2 if half else 4).wait_recv()
                first(part, c, 5 if half else 3).wait_recv()
                sums[half] = own1[part, c, half] + r1n[part, c, 0, half].astype(F32) + r1n[part, c, 1, half].astype(F32)
                if half:
                    s2[part, c, 1, 0] = sums[1][:64, :256].astype(BF16)
                    second(part, c, 0).start()
                    s2[part, c, 1, 1] = sums[1][64:, :256].astype(BF16)
                    second(part, c, 1).start()
                    s2[part, c, 2, 0] = sums[1][:64, 256:].astype(BF16)
                    second(part, c, 3).start()
                    s2[part, c, 2, 1] = sums[1][64:, 256:].astype(BF16)
                else:
                    s2[part, c, 0, 1] = sums[0][64:, 256:].astype(BF16)
                    second(part, c, 2).start()
                    s2[part, c, 0, 0] = sums[0][:64, 256:].astype(BF16)
                    acc[part, c] = sums[0][:, :256]

    def stage_pass2(c):
        for part in (0, 1):
            for way, (dp, half) in enumerate(((0, 0), (2, 1))):
                second(part, c, way).wait_recv()
                total = s2[part, c, dp, half].astype(F32) + r2o[part, c, way].astype(F32)
                s2[part, c, dp, half] = total.astype(BF16)
                second(part, c, 4 + way).start()

    def stage_last(c):
        for part in (0, 1):
            for half in (0, 1):
                second(part, c, 2 if half else 4).wait_recv()
                second(part, c, 5 if half else 3).wait_recv()
                acc[part, c, pl.ds(half * 64, 64)] += (
                    r2n[part, c, 0, half].astype(F32) + r2n[part, c, 1, half].astype(F32)
                )

    def step(t, _):
        @pl.when(t < CHUNKS - 1)
        def _():
            stage_states(t + 1)

        @pl.when(t < CHUNKS)
        def _():
            stage_project(t)

        @pl.when(t == 2)
        def _():
            final_copy.start()
            ss_in[...] = jnp.transpose(ssa[...])[:8]
            ss_core_copy().start()

        @pl.when(t == 3)
        def _():
            ss_core_copy().wait()
            ss_mid[0] = ss_in[...] + ss_core[...]
            for k in range(3):
                ss_x_copy(k).start()

        @pl.when(t == 4)
        def _():
            for k in range(3):
                ss_x_copy(k).wait()
            ss_mid[1] = ss_mid[0] + ss_x[0] + ss_x[1] + ss_x[2]
            for k in range(3):
                ss_y_copy(k).start()

        for lag, stage in ((1, stage_pass1), (2, stage_turn), (3, stage_pass2), (4, stage_last)):
            @pl.when(jnp.logical_and(t >= lag, t < CHUNKS + lag))
            def _():
                stage(t - lag)
        return 0

    stage_states(0)
    lax.fori_loop(0, CHUNKS + 4, step, 0)
    loads[5].wait()

    for k in range(3):
        ss_y_copy(k).wait()
    total = ss_mid[1] + ss_y[0] + ss_y[1] + ss_y[2]
    scale = lax.rsqrt(total / 16384.0 + 1e-05)
    scale = jnp.transpose(jnp.concatenate([scale] * 16, axis=0))
    for part in (0, 1):
        for c in range(CHUNKS):
            block = part * CHUNKS + c
            rows = pl.ds(block * SPAN, SPAN)
            out[rows, :] = (
                res[rows, :].astype(F32) + acc[part, c] * scale[:, block:block + 1]
            ).astype(BF16)

    def drain(c, _):
        for part in (0, 1):
            for kind in range(6):
                first(part, c, kind).wait_send()
                second(part, c, kind).wait_send()
        g_remote(c).wait_send()
        return 0

    lax.fori_loop(0, CHUNKS, drain, 0)
    for i, (dx, dy) in enumerate(ORDER):
        w_remote(i, dx, dy).wait_send()
    for k in range(3):
        req_copy(k).wait_send()
    for i in range(6):
        state_copy(i).wait_send()
    final_copy.wait()


def mixer(owner, slot, spans, decay, bias, skip, x, gate, step, sp, gain, w, res, cache):
    vmem = pl.BlockSpec(memory_space=pltpu.VMEM)
    smem = pl.BlockSpec(memory_space=pltpu.SMEM)
    hbm = pl.BlockSpec(memory_space=pl.ANY)
    dma = pltpu.SemaphoreType.DMA
    return pl.pallas_call(
        mixer_kernel,
        out_shape=(
            jax.ShapeDtypeStruct(res.shape, res.dtype),
            jax.ShapeDtypeStruct((2, 512, 256), F32),
        ),
        in_specs=[smem] * 6 + [hbm] * 8,
        out_specs=(vmem, hbm),
        scratch_shapes=[
            pltpu.VMEM((1024, 512), BF16),
            pltpu.VMEM((1024, 512), BF16),
            pltpu.VMEM((8, 1024), F32),
            pltpu.VMEM((8, 2, 1024, 256), BF16),
            pltpu.VMEM((1, 512), F32),
            pltpu.VMEM((1024, 256), BF16),
            pltpu.VMEM((64, 64, 256), BF16),
            pltpu.VMEM((8, 128), I32),
            pltpu.VMEM((3, 8, 128), I32),
            pltpu.SMEM((3, 8, 128), I32),
            pltpu.SMEM((3, 16), I32),
            pltpu.VMEM((18, 64, 256), BF16),
            pltpu.VMEM((18, 64, 256), BF16),
            pltpu.VMEM((2, 3, 64, 256), BF16),
            pltpu.VMEM((64, 128), F32),
            pltpu.VMEM((64, 128), F32),
            pltpu.VMEM((64, 128), F32),
            pltpu.VMEM((128, 1024), BF16),
            pltpu.VMEM((8, 128, 512), F32),
            pltpu.VMEM((8, 128, 512), F32),
            pltpu.VMEM((8, 512, 256), F32),
            pltpu.VMEM((8, 128, 256), BF16),
            pltpu.VMEM((2, 512, 256), F32),
            pltpu.VMEM((2, 512, 256), BF16),
            pltpu.VMEM((128, 128), F32),
            pltpu.VMEM((8, 128), F32),
            pltpu.VMEM((4, 4, 512, 256), BF16),
            pltpu.VMEM((4, 4, 512, 256), BF16),
            pltpu.VMEM((4, 256, 512), BF16),
            pltpu.VMEM((4, 256, 512), BF16),
            pltpu.VMEM((2, 4, 3, 2, 128, 512), BF16),
            pltpu.VMEM((2, 4, 2, 128, 512), F32),
            pltpu.VMEM((2, 4, 2, 128, 512), BF16),
            pltpu.VMEM((2, 4, 2, 2, 128, 512), BF16),
            pltpu.VMEM((2, 4, 3, 2, 64, 256), BF16),
            pltpu.VMEM((2, 4, 128, 256), F32),
            pltpu.VMEM((2, 4, 2, 64, 256), BF16),
            pltpu.VMEM((2, 4, 2, 2, 64, 256), BF16),
            pltpu.VMEM((2, 8, 128), F32),
            pltpu.VMEM((8, 128), F32),
            pltpu.VMEM((3, 8, 128), F32),
            pltpu.VMEM((3, 8, 128), F32),
            dma((6,)), dma((8,)), dma((3,)), dma((3,)), dma((3,)), dma((6,)), dma((6,)), dma(()),
            dma((16,)), dma((16,)), dma((16,)), dma((4,)), dma((4,)),
            dma((2, 4, 6)), dma((2, 4, 6)), dma((2, 4, 6)), dma((2, 4, 6)),
            dma((7,)), dma((7,)),
        ],
        compiler_params=pltpu.CompilerParams(
            collective_id=0, has_side_effects=True, vmem_limit_bytes=62 * 1024 * 1024
        ),
        cost_estimate=pl.CostEstimate(flops=10000000000, bytes_accessed=24000000, transcendentals=0),
        name="mixer",
    )(owner, slot, spans, decay, bias, skip, x, gate, step, sp, gain, w, res, cache)


def per_device(
    mixer_input, gate_input, step_raw, state_proj, decay_log, step_bias, skip_gain, norm_gain,
    out_weight, residual, new_spans, hit_owner, hit_slot, state_cache,
):
    mixed, final = mixer(
        hit_owner, hit_slot, new_spans, decay_log, step_bias, skip_gain,
        mixer_input, gate_input, step_raw.T, state_proj.reshape(2, 8192, 256),
        norm_gain.reshape(1, 512), out_weight, residual, state_cache.reshape(64, 64, 256),
    )
    return mixed, final.reshape(2, 8, 64, 256)


def solution(mesh):
    in_specs = (
        P("group", "head"),
        P("group", "head"),
        P("group", "head"),
        P(None, "group", None, None),
        P("head"),
        P("head"),
        P("head"),
        P("head"),
        P("head", None),
        P("group", "head"),
        P("group"),
        P("group", "head"),
        P("group", "head"),
        P("group", "head", None, None),
    )
    out_specs = (P("group", "head"), P("group", "head", None, None))
    return jax.shard_map(
        per_device, mesh=mesh, in_specs=in_specs, out_specs=out_specs, check_vma=False
    )
```

```python
import jax
import jax.numpy as jnp
from jax import lax
from jax.experimental import pallas as pl
from jax.experimental.pallas import tpu as pltpu
from jax.sharding import PartitionSpec as P

SPAN = 128
CAP = 6
UNITS = ((2, 1), (3, 1), (0, 1), (1, 1), (2, 0), (3, 0), (1, 0), (0, 0))
SIDE = 4
CHUNKS = 4
WEIGHTS_FIRST = False
BLOCKS = 8
MESH = pl.DeviceIdType.MESH
BF16 = jnp.bfloat16
F32 = jnp.float32
I32 = jnp.int32
HIGHEST = lax.Precision.HIGHEST


def remote(src, dst, send_sem, recv_sem, where):
    return pltpu.make_async_remote_copy(
        src_ref=src, dst_ref=dst, send_sem=send_sem, recv_sem=recv_sem,
        device_id=where, device_id_type=MESH,
    )


def dot_tn(a, b):
    return lax.dot_general(a, b, (((0,), (0,)), ((), ())), preferred_element_type=F32)


def dot_nt(a, b):
    return lax.dot_general(a, b, (((1,), (1,)), ((), ())), preferred_element_type=F32)


def mixer_kernel(
    owner_s, slot_s, spans_s, decay_s, bias_s, skip_s,
    x_hbm, gate_hbm, step_hbm, sp_hbm, gain_hbm, w_hbm, res_hbm, cache_hbm,
    out, state_out,
    x_v, gate_v, step_v, sp_v, gain_v, res, cache_v,
    req_v, rreq, req_s, idx_s, pbuf, rbuf, relay,
    e_v, f_v, em_v, sel_v, yi_v, ee_v, u_v, c_v, h_v, hb_v, ssa, ss_in,
    w_all, g_all, scale_v, s1, own1, r1o, r1n, s2, acc, r2o, r2n,
    ss_mid, ss_core, ss_x, ss_y,
    sem_in, sem_sp, sem_req_s, sem_req_r, sem_rs, sem_st_s, sem_st_r, sem_out,
    sem_w, sem_ws, sem_wr, sem_gs, sem_gr, sem_1s, sem_1r, sem_2s, sem_2r, sem_ss, sem_sr,
):
    me = lax.axis_index("head")
    deep = lax.axis_index("group")
    core = lax.rem(me, 2)
    col = lax.rem(me // 2, SIDE)
    row = me // (2 * SIDE)

    def head_at(dx, dy, dc):
        y = lax.rem(row + dy, SIDE)
        x = lax.rem(col + dx, SIDE)
        c = lax.rem(core + dc, 2)
        return (y * SIDE + x) * 2 + c

    def at_head(h):
        return {"head": h}

    partner = at_head(head_at(0, 0, 1))
    x_peers = [at_head(head_at(k, 0, 0)) for k in (1, 2, 3)]
    y_peers = [at_head(head_at(0, k, 0)) for k in (1, 2, 3)]
    z_peers = [{"group": lax.rem(deep + k, 4)} for k in (1, 2, 3)]
    p_side = ((x_peers[0], x_peers[2]), (y_peers[0], y_peers[2]))
    q_side = (p_side[1], p_side[0])

    barrier = pltpu.get_barrier_semaphore()
    for peer in z_peers + [partner] + x_peers + y_peers:
        pl.semaphore_signal(barrier, inc=1, device_id=peer, device_id_type=MESH)

    loads = [
        pltpu.make_async_copy(src, dst, sem_in.at[i])
        for i, (src, dst) in enumerate((
            (cache_hbm, cache_v), (step_hbm, step_v), (x_hbm, x_v), (gain_hbm, gain_v),
            (gate_hbm, gate_v), (res_hbm, res),
        ))
    ]

    def sp_copy(b):
        start = pl.multiple_of(b * 1024, 1024)
        return pltpu.make_async_copy(sp_hbm.at[:, pl.ds(start, 1024)], sp_v.at[b], sem_sp.at[b])

    def w_local(dx, dy):
        start = pl.multiple_of(head_at(dx, dy, 0) * 256, 256)
        dst = w_all.at[dx, pl.ds(0, 512), pl.ds(dy * 256, 256)]
        return pltpu.make_async_copy(w_hbm.at[:, pl.ds(start, 256)], dst, sem_w.at[dx, dy])

    def w_remote(dx, dy):
        start = pl.multiple_of(head_at(dx, dy, 1) * 256, 256)
        dst = w_all.at[dx, pl.ds(512, 512), pl.ds(dy * 256, 256)]
        return remote(w_hbm.at[:, pl.ds(start, 256)], dst, sem_ws.at[dx, dy], sem_wr.at[dx, dy], partner)

    def start_weights():
        for dx, dh in UNITS:
            for dy in (2 * dh, 2 * dh + 1):
                w_remote(dx, dy).start()
                w_local(dx, dy).start()
        loads[5].start()

    def g_remote(c):
        return remote(
            g_all.at[c, :, pl.ds(0, 512)], g_all.at[c, :, pl.ds(512, 512)], sem_gs.at[c], sem_gr.at[c], partner
        )

    for load in loads[:5]:
        load.start()
    for b in range(BLOCKS):
        sp_copy(b).start()

    lane = lax.broadcasted_iota(I32, (8, 128), 1)
    request = jnp.zeros((8, 128), I32)
    seen = jnp.zeros((8, 128), I32)
    counts = [jnp.int32(0)] * 4
    for e in range(16):
        s, j = divmod(e, 8)
        owner = owner_s[s, j]
        place = slot_s[s, j] * 8 + j
        named = (lane // 8) == owner
        request = jnp.where(jnp.logical_and(named, seen == lane % 8), place, request)
        seen = seen + jnp.where(named, 1, 0)
        rank = jnp.int32(0)
        for q in range(4):
            rank = jnp.where(owner == q, counts[q], rank)
            counts[q] = counts[q] + jnp.where(owner == q, 1, 0)
        away = lax.rem(owner - deep + 4, 4)
        idx_s[0, e] = jnp.where(away == 0, 0, (away - 1) * CAP + jnp.minimum(rank, CAP - 1))
        idx_s[1, e] = jnp.where(away == 0, 1, 0)
        idx_s[2, e] = place
    req_v[...] = request

    def req_copy(k):
        return remote(req_v, rreq.at[k], sem_req_s.at[k], sem_req_r.at[k], z_peers[k])

    pl.semaphore_wait(barrier, 10)
    for k in (1, 0, 2):
        req_copy(k).start()
    if WEIGHTS_FIRST:
        start_weights()

    sub = lax.broadcasted_iota(I32, (8, 128), 0)
    bias = jnp.zeros((8, 128), F32)
    decay = jnp.zeros((8, 128), F32)
    for j in range(8):
        bias = jnp.where(sub == j, bias_s[j], bias)
        decay = jnp.where(sub == j, decay_s[j], decay)
    decay = -jnp.exp(decay)
    loads[1].wait()
    steps = []
    for b in range(BLOCKS):
        raw = step_v[:, b * SPAN:(b + 1) * SPAN] + bias
        alive = jnp.where(b % CHUNKS < spans_s[b // CHUNKS], 1.0, 0.0)
        steps.append((jnp.maximum(raw, 0.0) + jnp.log1p(jnp.exp(-jnp.abs(raw)))) * alive)
    dt = jnp.concatenate(steps, axis=0)
    rate = jnp.concatenate([decay * step for step in steps], axis=0)
    square0 = lax.broadcasted_iota(I32, (SPAN, SPAN), 0)
    square1 = lax.broadcasted_iota(I32, (SPAN, SPAN), 1)
    upper = jnp.where(square0 <= square1, 1.0, 0.0).astype(F32)
    cum = jnp.dot(rate, upper, precision=HIGHEST, preferred_element_type=F32)
    middle = cum[:, SPAN - 1:] * 0.5
    e_v[...] = jnp.exp(cum - middle)
    f_v[...] = jnp.exp(middle - cum) * dt
    em_v[...] = jnp.exp(jnp.broadcast_to(middle, (BLOCKS * 8, 128)))
    ssa[...] = jnp.zeros((SPAN, SPAN), F32)

    def rank_copy(k):
        return pltpu.make_async_copy(rreq.at[k], req_s.at[k], sem_rs.at[k])

    def state_copy(i):
        src, dst, way = (
            (pbuf.at[pl.ds(6, 3)], relay.at[0], 0),
            (pbuf.at[pl.ds(9, 3)], relay.at[1], 2),
            (pbuf.at[pl.ds(0, 6)], rbuf.at[pl.ds(0, 6)], 2),
            (pbuf.at[pl.ds(12, 6)], rbuf.at[pl.ds(12, 6)], 0),
            (relay.at[0], rbuf.at[pl.ds(6, 3)], 0),
            (relay.at[1], rbuf.at[pl.ds(9, 3)], 2),
        )[i]
        return remote(src, dst, sem_st_s.at[i], sem_st_r.at[i], z_peers[way])

    loads[0].wait()
    for k in (1, 0, 2):
        req_copy(k).wait_recv()
        rank_copy(k).start()
    for k in (1, 0, 2):
        rank_copy(k).wait()
        for r in range(CAP):
            pbuf[k * CAP + r] = cache_v[req_s[k, 0, deep * 8 + r]]
            if k == 1 and r == 2:
                state_copy(0).start()
        state_copy((2, 1, 3)[k]).start()
    if not WEIGHTS_FIRST:
        start_weights()

    pick = me // 4
    sel_v[...] = jnp.where(
        lax.broadcasted_iota(I32, (SPAN, 1024), 1) == lax.broadcasted_iota(I32, (SPAN, 1024), 0) * 8 + pick, 1.0, 0.0
    ).astype(BF16)
    channel = lax.broadcasted_iota(I32, (16, 512), 1)
    spread = jnp.where(channel // 64 == lax.broadcasted_iota(I32, (16, 512), 0) % 8, 1.0, 0.0).astype(BF16)
    channel = lax.broadcasted_iota(I32, (1, 512), 1)
    skip = jnp.zeros((1, 512), F32)
    for j in range(8):
        skip = jnp.where(channel // 64 == j, skip_s[j], skip)
    for load in loads[2:5]:
        load.wait()

    def widen(part):
        high = part.astype(BF16)
        low = (part - high.astype(F32)).astype(BF16)
        return dot_tn(jnp.concatenate([high, low], axis=0), spread)

    def prepare(b, _):
        sp_copy(b).wait()
        few = pl.ds(pl.multiple_of(b * 8, 8), 8)
        x = x_v[pl.ds(pl.multiple_of(b * SPAN, SPAN), SPAN), :].astype(F32)
        wide_e = widen(e_v[few, :])
        ee_v[b] = wide_e
        z = (widen(f_v[few, :]) * x).astype(BF16)
        b_rows = jnp.dot(sel_v[...], sp_v[b, 0], preferred_element_type=F32).astype(BF16)
        c_rows = jnp.dot(sel_v[...], sp_v[b, 1], preferred_element_type=F32).astype(BF16)
        c_v[b] = c_rows
        scores = jnp.where(square0 >= square1, dot_nt(c_rows, b_rows), 0.0).astype(BF16)
        yi_v[b] = wide_e * jnp.dot(scores, z, preferred_element_type=F32) + skip * x
        u_v[b] = dot_tn(z, b_rows)

        @pl.when(b == 2)
        def _():
            for i in (0, 1):
                state_copy(i).wait_recv()
                state_copy(4 + i).start()
        return 0

    lax.fori_loop(0, BLOCKS, prepare, 0)

    for i in (2, 3, 4, 5):
        state_copy(i).wait_recv()
    for e in range(16):
        s, j = divmod(e, 8)
        here = cache_v[idx_s[2, e]].astype(F32)
        sent = rbuf[idx_s[0, e]].astype(F32)
        h_v[s, j * 64:(j + 1) * 64, :] = jnp.where(idx_s[1, e] == 1, here, sent)

    def stage_states(c):
        for s in (0, 1):
            b = s * CHUNKS + c
            for j in range(8):
                rows = slice(j * 64, (j + 1) * 64)
                fade = em_v[pl.ds(b * 8 + j, 1), :]
                fade = jnp.concatenate([fade, fade], axis=1)
                faded = h_v[s, rows, :] * fade
                hb_v[s, rows, :] = faded.astype(BF16)
                h_v[s, rows, :] = (faded + u_v[b, rows, :]) * fade
            y = yi_v[b] + ee_v[b] * dot_nt(c_v[b], hb_v[s])
            gate = gate_v[pl.ds(pl.multiple_of(b * SPAN, SPAN), SPAN), :].astype(F32)
            gated = y * (gate / (1.0 + jnp.exp(-gate)))
            ssa[...] = jnp.where(square1 == b, jnp.sum(gated * gated, axis=1, keepdims=True), ssa[...])
            g_all[c, s * SPAN:(s + 1) * SPAN, :512] = (gated * gain_v[...]).astype(BF16)
        g_remote(c).start()

    final_copy = pltpu.make_async_copy(h_v, state_out, sem_out)

    def ss_core_copy():
        return remote(ss_in, ss_core, sem_ss.at[0], sem_sr.at[0], partner)

    def ss_x_copy(k):
        return remote(ss_mid.at[0], ss_x.at[k], sem_ss.at[1 + k], sem_sr.at[1 + k], x_peers[k])

    def ss_y_copy(k):
        return remote(ss_mid.at[1], ss_y.at[k], sem_ss.at[4 + k], sem_sr.at[4 + k], y_peers[k])

    def first(part, c, kind):
        if kind == 0:
            src, dst, way = s1.at[part, c, 1, 0], r1o.at[part, c, 0], 0
        elif kind == 1:
            src, dst, way = s1.at[part, c, 1, 1], r1o.at[part, c, 1], 1
        elif kind == 2:
            src, dst, way = s1.at[part, c, 0, 1], r1n.at[part, c, 0, 1], 0
        elif kind == 3:
            src, dst, way = s1.at[part, c, 2, 0], r1n.at[part, c, 1, 0], 1
        elif kind == 4:
            src, dst, way = s1.at[part, c, 0, 0], r1n.at[part, c, 0, 0], 0
        else:
            src, dst, way = s1.at[part, c, 2, 1], r1n.at[part, c, 1, 1], 1
        return remote(src, dst, sem_1s.at[part, c, kind], sem_1r.at[part, c, kind], p_side[part][way])

    def second(part, c, kind):
        if kind == 0:
            src, dst, way = s2.at[part, c, 1, 0], r2o.at[part, c, 0], 0
        elif kind == 1:
            src, dst, way = s2.at[part, c, 1, 1], r2o.at[part, c, 1], 1
        elif kind == 2:
            src, dst, way = s2.at[part, c, 0, 1], r2n.at[part, c, 0, 1], 0
        elif kind == 3:
            src, dst, way = s2.at[part, c, 2, 0], r2n.at[part, c, 1, 0], 1
        elif kind == 4:
            src, dst, way = s2.at[part, c, 0, 0], r2n.at[part, c, 0, 0], 0
        else:
            src, dst, way = s2.at[part, c, 2, 1], r2n.at[part, c, 1, 1], 1
        return remote(src, dst, sem_2s.at[part, c, kind], sem_2r.at[part, c, kind], q_side[part][way])

    IMMEDIATE = {(2, 0): 0, (2, 1): 1, (1, 1): 2, (3, 0): 3}

    def stage_project(c):
        g_remote(c).wait_recv()
        done = set()
        for dx, dh in UNITS:
            @pl.when(c == 0)
            def _():
                for dy in (2 * dh, 2 * dh + 1):
                    w_local(dx, dy).wait()
                    w_remote(dx, dy).wait_recv()
            term = jnp.dot(g_all[c], w_all[dx, :, dh * 512:(dh + 1) * 512], preferred_element_type=F32)
            for dy in (2 * dh, 2 * dh + 1):
                for part, dp, dq in ((0, dx, dy), (1, dy, dx)):
                    piece = term[part * SPAN:(part + 1) * SPAN, (dy % 2) * 256:(dy % 2 + 1) * 256]
                    columns = pl.ds((dq % 2) * 256, 256)
                    if dp == 0:
                        own1[part, c, dq // 2, :, columns] = piece
                    else:
                        s1[part, c, dp - 1, dq // 2, :, columns] = piece.astype(BF16)
            for dy in (2 * dh, 2 * dh + 1):
                for part, dp, dq in ((0, dx, dy), (1, dy, dx)):
                    done.add((part, dp, dq))
                    kind = IMMEDIATE.get((dp, dq // 2))
                    if kind is not None and (part, dp, dq ^ 1) in done:
                        first(part, c, kind).start()

    def stage_pass1(c):
        for part in (0, 1):
            for way, (dp, half) in enumerate(((0, 0), (2, 1))):
                first(part, c, way).wait_recv()
                total = s1[part, c, dp, half].astype(F32) + r1o[part, c, way].astype(F32)
                s1[part, c, dp, half] = total.astype(BF16)
                first(part, c, 4 + way).start()

    def stage_turn(c):
        for part in (0, 1):
            sums = [None, None]
            for half in (1, 0):
                first(part, c, 2 if half else 4).wait_recv()
                first(part, c, 5 if half else 3).wait_recv()
                sums[half] = own1[part, c, half] + r1n[part, c, 0, half].astype(F32) + r1n[part, c, 1, half].astype(F32)
                if half:
                    s2[part, c, 1, 0] = sums[1][:64, :256].astype(BF16)
                    second(part, c, 0).start()
                    s2[part, c, 1, 1] = sums[1][64:, :256].astype(BF16)
                    second(part, c, 1).start()
                    s2[part, c, 2, 0] = sums[1][:64, 256:].astype(BF16)
                    second(part, c, 3).start()
                    s2[part, c, 2, 1] = sums[1][64:, 256:].astype(BF16)
                else:
                    s2[part, c, 0, 1] = sums[0][64:, 256:].astype(BF16)
                    second(part, c, 2).start()
                    s2[part, c, 0, 0] = sums[0][:64, 256:].astype(BF16)
                    acc[part, c] = sums[0][:, :256]

    def stage_pass2(c):
        for part in (0, 1):
            for way, (dp, half) in enumerate(((0, 0), (2, 1))):
                second(part, c, way).wait_recv()
                total = s2[part, c, dp, half].astype(F32) + r2o[part, c, way].astype(F32)
                s2[part, c, dp, half] = total.astype(BF16)
                second(part, c, 4 + way).start()

    def stage_last(c):
        for part in (0, 1):
            for half in (0, 1):
                second(part, c, 2 if half else 4).wait_recv()
                second(part, c, 5 if half else 3).wait_recv()
                acc[part, c, pl.ds(half * 64, 64)] += (
                    r2n[part, c, 0, half].astype(F32) + r2n[part, c, 1, half].astype(F32)
                )

    def finish(c):
        for part in (0, 1):
            b = part * CHUNKS + c
            rows = pl.ds(pl.multiple_of(b * SPAN, SPAN), SPAN)
            scale = jnp.sum(jnp.where(square1 == b, scale_v[...], 0.0), axis=1, keepdims=True)
            out[rows, :] = (res[rows, :].astype(F32) + acc[part, c] * scale).astype(BF16)

    def step(t, _):
        @pl.when(t < CHUNKS - 1)
        def _():
            stage_states(t + 1)

        @pl.when(t < CHUNKS)
        def _():
            stage_project(t)

        @pl.when(t == 2)
        def _():
            final_copy.start()
            ss_in[...] = jnp.transpose(ssa[...])[:8]
            ss_core_copy().start()

        @pl.when(t == 3)
        def _():
            ss_core_copy().wait()
            ss_mid[0] = ss_in[...] + ss_core[...]
            for k in range(3):
                ss_x_copy(k).start()

        @pl.when(t == 4)
        def _():
            for k in range(3):
                ss_x_copy(k).wait()
            ss_mid[1] = ss_mid[0] + ss_x[0] + ss_x[1] + ss_x[2]
            for k in range(3):
                ss_y_copy(k).start()

        for lag, stage in ((1, stage_pass1), (2, stage_turn), (3, stage_pass2), (4, stage_last)):
            @pl.when(jnp.logical_and(t >= lag, t < CHUNKS + lag))
            def _():
                stage(t - lag)

        @pl.when(t == 5)
        def _():
            for k in range(3):
                ss_y_copy(k).wait()
            loads[5].wait()
            total = ss_mid[1] + ss_y[0] + ss_y[1] + ss_y[2]
            scale = lax.rsqrt(total / 16384.0 + 1e-05)
            scale_v[...] = jnp.transpose(jnp.concatenate([scale] * 16, axis=0))
            finish(0)

        @pl.when(t >= 5)
        def _():
            finish(t - 4)
        return 0

    stage_states(0)
    lax.fori_loop(0, CHUNKS + 4, step, 0)

    def drain(c, _):
        for part in (0, 1):
            for kind in range(6):
                first(part, c, kind).wait_send()
                second(part, c, kind).wait_send()
        g_remote(c).wait_send()
        return 0

    lax.fori_loop(0, CHUNKS, drain, 0)
    for dx, dh in UNITS:
        for dy in (2 * dh, 2 * dh + 1):
            w_remote(dx, dy).wait_send()
    for k in range(3):
        req_copy(k).wait_send()
    for i in range(6):
        state_copy(i).wait_send()
    final_copy.wait()


def mixer(owner, slot, spans, decay, bias, skip, x, gate, step, sp, gain, w, res, cache):
    vmem = pl.BlockSpec(memory_space=pltpu.VMEM)
    smem = pl.BlockSpec(memory_space=pltpu.SMEM)
    hbm = pl.BlockSpec(memory_space=pl.ANY)
    dma = pltpu.SemaphoreType.DMA
    return pl.pallas_call(
        mixer_kernel,
        out_shape=(
            jax.ShapeDtypeStruct(res.shape, res.dtype),
            jax.ShapeDtypeStruct((2, 512, 256), F32),
        ),
        in_specs=[smem] * 6 + [hbm] * 8,
        out_specs=(vmem, hbm),
        scratch_shapes=[
            pltpu.VMEM((1024, 512), BF16),
            pltpu.VMEM((1024, 512), BF16),
            pltpu.VMEM((8, 1024), F32),
            pltpu.VMEM((8, 2, 1024, 256), BF16),
            pltpu.VMEM((1, 512), F32),
            pltpu.VMEM((1024, 256), BF16),
            pltpu.VMEM((64, 64, 256), BF16),
            pltpu.VMEM((8, 128), I32),
            pltpu.VMEM((3, 8, 128), I32),
            pltpu.SMEM((3, 8, 128), I32),
            pltpu.SMEM((3, 16), I32),
            pltpu.VMEM((18, 64, 256), BF16),
            pltpu.VMEM((18, 64, 256), BF16),
            pltpu.VMEM((2, 3, 64, 256), BF16),
            pltpu.VMEM((64, 128), F32),
            pltpu.VMEM((64, 128), F32),
            pltpu.VMEM((64, 128), F32),
            pltpu.VMEM((128, 1024), BF16),
            pltpu.VMEM((8, 128, 512), F32),
            pltpu.VMEM((8, 128, 512), F32),
            pltpu.VMEM((8, 512, 256), F32),
            pltpu.VMEM((8, 128, 256), BF16),
            pltpu.VMEM((2, 512, 256), F32),
            pltpu.VMEM((2, 512, 256), BF16),
            pltpu.VMEM((128, 128), F32),
            pltpu.VMEM((8, 128), F32),
            pltpu.VMEM((4, 1024, 1024), BF16),
            pltpu.VMEM((4, 256, 1024), BF16),
            pltpu.VMEM((128, 128), F32),
            pltpu.VMEM((2, 4, 3, 2, 128, 512), BF16),
            pltpu.VMEM((2, 4, 2, 128, 512), F32),
            pltpu.VMEM((2, 4, 2, 128, 512), BF16),
            pltpu.VMEM((2, 4, 2, 2, 128, 512), BF16),
            pltpu.VMEM((2, 4, 3, 2, 64, 256), BF16),
            pltpu.VMEM((2, 4, 128, 256), F32),
            pltpu.VMEM((2, 4, 2, 64, 256), BF16),
            pltpu.VMEM((2, 4, 2, 2, 64, 256), BF16),
            pltpu.VMEM((2, 8, 128), F32),
            pltpu.VMEM((8, 128), F32),
            pltpu.VMEM((3, 8, 128), F32),
            pltpu.VMEM((3, 8, 128), F32),
            dma((6,)), dma((8,)), dma((3,)), dma((3,)), dma((3,)), dma((6,)), dma((6,)), dma(()),
            dma((4, 4)), dma((4, 4)), dma((4, 4)), dma((4,)), dma((4,)),
            dma((2, 4, 6)), dma((2, 4, 6)), dma((2, 4, 6)), dma((2, 4, 6)),
            dma((7,)), dma((7,)),
        ],
        compiler_params=pltpu.CompilerParams(
            collective_id=0, has_side_effects=True, vmem_limit_bytes=62 * 1024 * 1024
        ),
        cost_estimate=pl.CostEstimate(flops=10000000000, bytes_accessed=24000000, transcendentals=0),
        name="mixer",
    )(owner, slot, spans, decay, bias, skip, x, gate, step, sp, gain, w, res, cache)


def per_device(
    mixer_input, gate_input, step_raw, state_proj, decay_log, step_bias, skip_gain, norm_gain,
    out_weight, residual, new_spans, hit_owner, hit_slot, state_cache,
):
    mixed, final = mixer(
        hit_owner, hit_slot, new_spans, decay_log, step_bias, skip_gain,
        mixer_input, gate_input, step_raw.T, state_proj.reshape(2, 8192, 256),
        norm_gain.reshape(1, 512), out_weight, residual, state_cache.reshape(64, 64, 256),
    )
    return mixed, final.reshape(2, 8, 64, 256)


def solution(mesh):
    in_specs = (
        P("group", "head"),
        P("group", "head"),
        P("group", "head"),
        P(None, "group", None, None),
        P("head"),
        P("head"),
        P("head"),
        P("head"),
        P("head", None),
        P("group", "head"),
        P("group"),
        P("group", "head"),
        P("group", "head"),
        P("group", "head", None, None),
    )
    out_specs = (P("group", "head"), P("group", "head", None, None))
    return jax.shard_map(
        per_device, mesh=mesh, in_specs=in_specs, out_specs=out_specs, check_vma=False
    )
```

```python
import jax
import jax.numpy as jnp
from jax import lax
from jax.experimental import pallas as pl
from jax.experimental.pallas import tpu as pltpu
from jax.sharding import PartitionSpec as P

SPAN = 128
CAP = 6
UNITS = ((2, 1), (3, 1), (0, 1), (1, 1), (2, 0), (3, 0), (1, 0), (0, 0))
SIDE = 4
CHUNKS = 4
WEIGHTS_FIRST = False
BLOCKS = 8
MESH = pl.DeviceIdType.MESH
BF16 = jnp.bfloat16
F32 = jnp.float32
I32 = jnp.int32
HIGHEST = lax.Precision.HIGHEST


def remote(src, dst, send_sem, recv_sem, where):
    return pltpu.make_async_remote_copy(
        src_ref=src, dst_ref=dst, send_sem=send_sem, recv_sem=recv_sem,
        device_id=where, device_id_type=MESH,
    )


def dot_tn(a, b):
    return lax.dot_general(a, b, (((0,), (0,)), ((), ())), preferred_element_type=F32)


def dot_nt(a, b):
    return lax.dot_general(a, b, (((1,), (1,)), ((), ())), preferred_element_type=F32)


def mixer_kernel(
    owner_hbm, slot_hbm, spans_hbm, decay_hbm, bias_hbm, skip_hbm,
    x_hbm, gate_hbm, step_hbm, sp_hbm, gain_hbm, w_hbm, res_hbm, cache_hbm,
    out, h_v,
    owner_s, slot_s, spans_s, decay_s, bias_s, skip_s,
    x_v, gate_v, step_v, sp_v, gain_v, res, cache_v,
    req_v, rreq, req_s, idx_s, pbuf, rbuf, relay,
    e_v, f_v, em_v, sel_v, yi_v, ee_v, u_v, c_v, hb_v, ssa, ss_in,
    w_all, g_all, scale_v, s1, own1, r1o, r1n, s2, acc, r2o, r2n,
    ss_mid, ss_core, ss_x, ss_y,
    sem_in, sem_sp, sem_req_s, sem_req_r, sem_rs, sem_st_s, sem_st_r, sem_sc,
    sem_w, sem_ws, sem_wr, sem_gs, sem_gr, sem_1s, sem_1r, sem_2s, sem_2r, sem_ss, sem_sr,
):
    me = lax.axis_index("head")
    deep = lax.axis_index("group")
    core = lax.rem(me, 2)
    col = lax.rem(me // 2, SIDE)
    row = me // (2 * SIDE)

    def head_at(dx, dy, dc):
        y = lax.rem(row + dy, SIDE)
        x = lax.rem(col + dx, SIDE)
        c = lax.rem(core + dc, 2)
        return (y * SIDE + x) * 2 + c

    def at_head(h):
        return {"head": h}

    partner = at_head(head_at(0, 0, 1))
    x_peers = [at_head(head_at(k, 0, 0)) for k in (1, 2, 3)]
    y_peers = [at_head(head_at(0, k, 0)) for k in (1, 2, 3)]
    z_peers = [{"group": lax.rem(deep + k, 4)} for k in (1, 2, 3)]
    p_side = ((x_peers[0], x_peers[2]), (y_peers[0], y_peers[2]))
    q_side = (p_side[1], p_side[0])

    barrier = pltpu.get_barrier_semaphore()
    for peer in z_peers + [partner] + x_peers + y_peers:
        pl.semaphore_signal(barrier, inc=1, device_id=peer, device_id_type=MESH)

    loads = [
        pltpu.make_async_copy(src, dst, sem_in.at[i])
        for i, (src, dst) in enumerate((
            (cache_hbm, cache_v), (step_hbm, step_v), (x_hbm, x_v), (gain_hbm, gain_v),
            (gate_hbm, gate_v), (res_hbm, res),
        ))
    ]

    def sp_copy(b):
        start = pl.multiple_of(b * 1024, 1024)
        return pltpu.make_async_copy(sp_hbm.at[:, pl.ds(start, 1024)], sp_v.at[b], sem_sp.at[b])

    def w_local(dx, dy):
        start = pl.multiple_of(head_at(dx, dy, 0) * 256, 256)
        dst = w_all.at[dx, pl.ds(0, 512), pl.ds(dy * 256, 256)]
        return pltpu.make_async_copy(w_hbm.at[:, pl.ds(start, 256)], dst, sem_w.at[dx, dy])

    def w_remote(dx, dy):
        start = pl.multiple_of(head_at(dx, dy, 1) * 256, 256)
        dst = w_all.at[dx, pl.ds(512, 512), pl.ds(dy * 256, 256)]
        return remote(w_hbm.at[:, pl.ds(start, 256)], dst, sem_ws.at[dx, dy], sem_wr.at[dx, dy], partner)

    def start_weights():
        for dx, dh in UNITS:
            for dy in (2 * dh, 2 * dh + 1):
                w_remote(dx, dy).start()
                w_local(dx, dy).start()
        loads[5].start()

    def g_remote(c):
        return remote(
            g_all.at[c, :, pl.ds(0, 512)], g_all.at[c, :, pl.ds(512, 512)], sem_gs.at[c], sem_gr.at[c], partner
        )

    scalars = [
        pltpu.make_async_copy(src, dst, sem_sc.at[i])
        for i, (src, dst) in enumerate((
            (owner_hbm, owner_s), (slot_hbm, slot_s), (spans_hbm, spans_s),
            (decay_hbm, decay_s), (bias_hbm, bias_s), (skip_hbm, skip_s),
        ))
    ]
    for scalar in scalars:
        scalar.start()
    for load in loads[:5]:
        load.start()
    for b in range(BLOCKS):
        sp_copy(b).start()

    for scalar in scalars:
        scalar.wait()

    lane = lax.broadcasted_iota(I32, (8, 128), 1)
    request = jnp.zeros((8, 128), I32)
    seen = jnp.zeros((8, 128), I32)
    counts = [jnp.int32(0)] * 4
    for e in range(16):
        s, j = divmod(e, 8)
        owner = owner_s[s, j]
        place = slot_s[s, j] * 8 + j
        named = (lane // 8) == owner
        request = jnp.where(jnp.logical_and(named, seen == lane % 8), place, request)
        seen = seen + jnp.where(named, 1, 0)
        rank = jnp.int32(0)
        for q in range(4):
            rank = jnp.where(owner == q, counts[q], rank)
            counts[q] = counts[q] + jnp.where(owner == q, 1, 0)
        away = lax.rem(owner - deep + 4, 4)
        idx_s[0, e] = jnp.where(away == 0, 0, (away - 1) * CAP + jnp.minimum(rank, CAP - 1))
        idx_s[1, e] = jnp.where(away == 0, 1, 0)
        idx_s[2, e] = place
    req_v[...] = request

    def req_copy(k):
        return remote(req_v, rreq.at[k], sem_req_s.at[k], sem_req_r.at[k], z_peers[k])

    pl.semaphore_wait(barrier, 10)
    for k in (1, 0, 2):
        req_copy(k).start()
    if WEIGHTS_FIRST:
        start_weights()

    sub = lax.broadcasted_iota(I32, (8, 128), 0)
    bias = jnp.zeros((8, 128), F32)
    decay = jnp.zeros((8, 128), F32)
    for j in range(8):
        bias = jnp.where(sub == j, bias_s[j], bias)
        decay = jnp.where(sub == j, decay_s[j], decay)
    decay = -jnp.exp(decay)
    loads[1].wait()
    steps = []
    for b in range(BLOCKS):
        raw = step_v[:, b * SPAN:(b + 1) * SPAN] + bias
        alive = jnp.where(b % CHUNKS < spans_s[b // CHUNKS], 1.0, 0.0)
        steps.append((jnp.maximum(raw, 0.0) + jnp.log1p(jnp.exp(-jnp.abs(raw)))) * alive)
    dt = jnp.concatenate(steps, axis=0)
    rate = jnp.concatenate([decay * step for step in steps], axis=0)
    square0 = lax.broadcasted_iota(I32, (SPAN, SPAN), 0)
    square1 = lax.broadcasted_iota(I32, (SPAN, SPAN), 1)
    upper = jnp.where(square0 <= square1, 1.0, 0.0).astype(F32)
    cum = jnp.dot(rate, upper, precision=HIGHEST, preferred_element_type=F32)
    middle = cum[:, SPAN - 1:] * 0.5
    e_v[...] = jnp.exp(cum - middle)
    f_v[...] = jnp.exp(middle - cum) * dt
    em_v[...] = jnp.exp(jnp.broadcast_to(middle, (BLOCKS * 8, 128)))
    ssa[...] = jnp.zeros((SPAN, SPAN), F32)

    def rank_copy(k):
        return pltpu.make_async_copy(rreq.at[k], req_s.at[k], sem_rs.at[k])

    def state_copy(i):
        src, dst, way = (
            (pbuf.at[pl.ds(6, 3)], relay.at[0], 0),
            (pbuf.at[pl.ds(9, 3)], relay.at[1], 2),
            (pbuf.at[pl.ds(0, 6)], rbuf.at[pl.ds(0, 6)], 2),
            (pbuf.at[pl.ds(12, 6)], rbuf.at[pl.ds(12, 6)], 0),
            (relay.at[0], rbuf.at[pl.ds(6, 3)], 0),
            (relay.at[1], rbuf.at[pl.ds(9, 3)], 2),
        )[i]
        return remote(src, dst, sem_st_s.at[i], sem_st_r.at[i], z_peers[way])

    loads[0].wait()
    for k in (1, 0, 2):
        req_copy(k).wait_recv()
        rank_copy(k).start()
    for k in (1, 0, 2):
        rank_copy(k).wait()
        for r in range(CAP):
            pbuf[k * CAP + r] = cache_v[req_s[k, 0, deep * 8 + r]]
            if k == 1 and r == 2:
                state_copy(0).start()
        state_copy((2, 1, 3)[k]).start()
    if not WEIGHTS_FIRST:
        start_weights()

    pick = me // 4
    sel_v[...] = jnp.where(
        lax.broadcasted_iota(I32, (SPAN, 1024), 1) == lax.broadcasted_iota(I32, (SPAN, 1024), 0) * 8 + pick, 1.0, 0.0
    ).astype(BF16)
    channel = lax.broadcasted_iota(I32, (16, 512), 1)
    spread = jnp.where(channel // 64 == lax.broadcasted_iota(I32, (16, 512), 0) % 8, 1.0, 0.0).astype(BF16)
    channel = lax.broadcasted_iota(I32, (1, 512), 1)
    skip = jnp.zeros((1, 512), F32)
    for j in range(8):
        skip = jnp.where(channel // 64 == j, skip_s[j], skip)
    for load in loads[2:5]:
        load.wait()

    def widen(part):
        high = part.astype(BF16)
        low = (part - high.astype(F32)).astype(BF16)
        return dot_tn(jnp.concatenate([high, low], axis=0), spread)

    def prepare(b, _):
        sp_copy(b).wait()
        few = pl.ds(pl.multiple_of(b * 8, 8), 8)
        x = x_v[pl.ds(pl.multiple_of(b * SPAN, SPAN), SPAN), :].astype(F32)
        wide_e = widen(e_v[few, :])
        ee_v[b] = wide_e
        z = (widen(f_v[few, :]) * x).astype(BF16)
        b_rows = jnp.dot(sel_v[...], sp_v[b, 0], preferred_element_type=F32).astype(BF16)
        c_rows = jnp.dot(sel_v[...], sp_v[b, 1], preferred_element_type=F32).astype(BF16)
        c_v[b] = c_rows
        scores = jnp.where(square0 >= square1, dot_nt(c_rows, b_rows), 0.0).astype(BF16)
        yi_v[b] = wide_e * jnp.dot(scores, z, preferred_element_type=F32) + skip * x
        u_v[b] = dot_tn(z, b_rows)

        @pl.when(b == 2)
        def _():
            for i in (0, 1):
                state_copy(i).wait_recv()
                state_copy(4 + i).start()
        return 0

    lax.fori_loop(0, BLOCKS, prepare, 0)

    for i in (2, 3, 4, 5):
        state_copy(i).wait_recv()
    for e in range(16):
        s, j = divmod(e, 8)
        here = cache_v[idx_s[2, e]].astype(F32)
        sent = rbuf[idx_s[0, e]].astype(F32)
        h_v[s, j * 64:(j + 1) * 64, :] = jnp.where(idx_s[1, e] == 1, here, sent)

    def stage_states(c):
        for s in (0, 1):
            b = s * CHUNKS + c
            for j in range(8):
                rows = slice(j * 64, (j + 1) * 64)
                fade = em_v[pl.ds(b * 8 + j, 1), :]
                fade = jnp.concatenate([fade, fade], axis=1)
                faded = h_v[s, rows, :] * fade
                hb_v[s, rows, :] = faded.astype(BF16)
                h_v[s, rows, :] = (faded + u_v[b, rows, :]) * fade
            y = yi_v[b] + ee_v[b] * dot_nt(c_v[b], hb_v[s])
            gate = gate_v[pl.ds(pl.multiple_of(b * SPAN, SPAN), SPAN), :].astype(F32)
            gated = y * (gate / (1.0 + jnp.exp(-gate)))
            ssa[...] = jnp.where(square1 == b, jnp.sum(gated * gated, axis=1, keepdims=True), ssa[...])
            g_all[c, s * SPAN:(s + 1) * SPAN, :512] = (gated * gain_v[...]).astype(BF16)
        g_remote(c).start()


    def ss_core_copy():
        return remote(ss_in, ss_core, sem_ss.at[0], sem_sr.at[0], partner)

    def ss_x_copy(k):
        return remote(ss_mid.at[0], ss_x.at[k], sem_ss.at[1 + k], sem_sr.at[1 + k], x_peers[k])

    def ss_y_copy(k):
        return remote(ss_mid.at[1], ss_y.at[k], sem_ss.at[4 + k], sem_sr.at[4 + k], y_peers[k])

    def first(part, c, kind):
        if kind == 0:
            src, dst, way = s1.at[part, c, 1, 0], r1o.at[part, c, 0], 0
        elif kind == 1:
            src, dst, way = s1.at[part, c, 1, 1], r1o.at[part, c, 1], 1
        elif kind == 2:
            src, dst, way = s1.at[part, c, 0, 1], r1n.at[part, c, 0, 1], 0
        elif kind == 3:
            src, dst, way = s1.at[part, c, 2, 0], r1n.at[part, c, 1, 0], 1
        elif kind == 4:
            src, dst, way = s1.at[part, c, 0, 0], r1n.at[part, c, 0, 0], 0
        else:
            src, dst, way = s1.at[part, c, 2, 1], r1n.at[part, c, 1, 1], 1
        return remote(src, dst, sem_1s.at[part, c, kind], sem_1r.at[part, c, kind], p_side[part][way])

    def second(part, c, kind):
        if kind == 0:
            src, dst, way = s2.at[part, c, 1, 0], r2o.at[part, c, 0], 0
        elif kind == 1:
            src, dst, way = s2.at[part, c, 1, 1], r2o.at[part, c, 1], 1
        elif kind == 2:
            src, dst, way = s2.at[part, c, 0, 1], r2n.at[part, c, 0, 1], 0
        elif kind == 3:
            src, dst, way = s2.at[part, c, 2, 0], r2n.at[part, c, 1, 0], 1
        elif kind == 4:
            src, dst, way = s2.at[part, c, 0, 0], r2n.at[part, c, 0, 0], 0
        else:
            src, dst, way = s2.at[part, c, 2, 1], r2n.at[part, c, 1, 1], 1
        return remote(src, dst, sem_2s.at[part, c, kind], sem_2r.at[part, c, kind], q_side[part][way])

    IMMEDIATE = {(2, 0): 0, (2, 1): 1, (1, 1): 2, (3, 0): 3}

    def stage_project(c):
        g_remote(c).wait_recv()
        done = set()
        for dx, dh in UNITS:
            @pl.when(c == 0)
            def _():
                for dy in (2 * dh, 2 * dh + 1):
                    w_local(dx, dy).wait()
                    w_remote(dx, dy).wait_recv()
            term = jnp.dot(g_all[c], w_all[dx, :, dh * 512:(dh + 1) * 512], preferred_element_type=F32)
            for dy in (2 * dh, 2 * dh + 1):
                for part, dp, dq in ((0, dx, dy), (1, dy, dx)):
                    piece = term[part * SPAN:(part + 1) * SPAN, (dy % 2) * 256:(dy % 2 + 1) * 256]
                    columns = pl.ds((dq % 2) * 256, 256)
                    if dp == 0:
                        own1[part, c, dq // 2, :, columns] = piece
                    else:
                        s1[part, c, dp - 1, dq // 2, :, columns] = piece.astype(BF16)
            for dy in (2 * dh, 2 * dh + 1):
                for part, dp, dq in ((0, dx, dy), (1, dy, dx)):
                    done.add((part, dp, dq))
                    kind = IMMEDIATE.get((dp, dq // 2))
                    if kind is not None and (part, dp, dq ^ 1) in done:
                        first(part, c, kind).start()

    def stage_pass1(c):
        for part in (0, 1):
            for way, (dp, half) in enumerate(((0, 0), (2, 1))):
                first(part, c, way).wait_recv()
                total = s1[part, c, dp, half].astype(F32) + r1o[part, c, way].astype(F32)
                s1[part, c, dp, half] = total.astype(BF16)
                first(part, c, 4 + way).start()

    def stage_turn(c):
        for part in (0, 1):
            sums = [None, None]
            for half in (1, 0):
                first(part, c, 2 if half else 4).wait_recv()
                first(part, c, 5 if half else 3).wait_recv()
                sums[half] = own1[part, c, half] + r1n[part, c, 0, half].astype(F32) + r1n[part, c, 1, half].astype(F32)
                if half:
                    s2[part, c, 1, 0] = sums[1][:64, :256].astype(BF16)
                    second(part, c, 0).start()
                    s2[part, c, 1, 1] = sums[1][64:, :256].astype(BF16)
                    second(part, c, 1).start()
                    s2[part, c, 2, 0] = sums[1][:64, 256:].astype(BF16)
                    second(part, c, 3).start()
                    s2[part, c, 2, 1] = sums[1][64:, 256:].astype(BF16)
                else:
                    s2[part, c, 0, 1] = sums[0][64:, 256:].astype(BF16)
                    second(part, c, 2).start()
                    s2[part, c, 0, 0] = sums[0][:64, 256:].astype(BF16)
                    acc[part, c] = sums[0][:, :256]

    def stage_pass2(c):
        for part in (0, 1):
            for way, (dp, half) in enumerate(((0, 0), (2, 1))):
                second(part, c, way).wait_recv()
                total = s2[part, c, dp, half].astype(F32) + r2o[part, c, way].astype(F32)
                s2[part, c, dp, half] = total.astype(BF16)
                second(part, c, 4 + way).start()

    def stage_last(c):
        for part in (0, 1):
            for half in (0, 1):
                second(part, c, 2 if half else 4).wait_recv()
                second(part, c, 5 if half else 3).wait_recv()
                acc[part, c, pl.ds(half * 64, 64)] += (
                    r2n[part, c, 0, half].astype(F32) + r2n[part, c, 1, half].astype(F32)
                )

    def finish(c):
        for part in (0, 1):
            b = part * CHUNKS + c
            rows = pl.ds(pl.multiple_of(b * SPAN, SPAN), SPAN)
            scale = jnp.sum(jnp.where(square1 == b, scale_v[...], 0.0), axis=1, keepdims=True)
            out[rows, :] = (res[rows, :].astype(F32) + acc[part, c] * scale).astype(BF16)

    def step(t, _):
        @pl.when(t < CHUNKS - 1)
        def _():
            stage_states(t + 1)

        @pl.when(t < CHUNKS)
        def _():
            stage_project(t)

        @pl.when(t == 2)
        def _():
            ss_in[...] = jnp.transpose(ssa[...])[:8]
            ss_core_copy().start()

        @pl.when(t == 3)
        def _():
            ss_core_copy().wait()
            ss_mid[0] = ss_in[...] + ss_core[...]
            for k in range(3):
                ss_x_copy(k).start()

        @pl.when(t == 4)
        def _():
            for k in range(3):
                ss_x_copy(k).wait()
            ss_mid[1] = ss_mid[0] + ss_x[0] + ss_x[1] + ss_x[2]
            for k in range(3):
                ss_y_copy(k).start()

        for lag, stage in ((1, stage_pass1), (2, stage_turn), (3, stage_pass2), (4, stage_last)):
            @pl.when(jnp.logical_and(t >= lag, t < CHUNKS + lag))
            def _():
                stage(t - lag)

        @pl.when(t == 5)
        def _():
            for k in range(3):
                ss_y_copy(k).wait()
            loads[5].wait()
            total = ss_mid[1] + ss_y[0] + ss_y[1] + ss_y[2]
            scale = lax.rsqrt(total / 16384.0 + 1e-05)
            scale_v[...] = jnp.transpose(jnp.concatenate([scale] * 16, axis=0))
            finish(0)

        @pl.when(t >= 5)
        def _():
            finish(t - 4)
        return 0

    stage_states(0)
    lax.fori_loop(0, CHUNKS + 4, step, 0)

    def drain(c, _):
        for part in (0, 1):
            for kind in range(6):
                first(part, c, kind).wait_send()
                second(part, c, kind).wait_send()
        g_remote(c).wait_send()
        return 0

    lax.fori_loop(0, CHUNKS, drain, 0)
    for dx, dh in UNITS:
        for dy in (2 * dh, 2 * dh + 1):
            w_remote(dx, dy).wait_send()
    for k in range(3):
        req_copy(k).wait_send()
    for i in range(6):
        state_copy(i).wait_send()


def mixer(owner, slot, spans, decay, bias, skip, x, gate, step, sp, gain, w, res, cache):
    vmem = pl.BlockSpec(memory_space=pltpu.VMEM)
    hbm = pl.BlockSpec(memory_space=pl.ANY)
    dma = pltpu.SemaphoreType.DMA
    return pl.pallas_call(
        mixer_kernel,
        out_shape=(
            pltpu.VMEM(res.shape, res.dtype),
            pltpu.VMEM((2, 512, 256), F32),
        ),
        in_specs=[hbm] * 14,
        out_specs=(vmem, vmem),
        scratch_shapes=[
            pltpu.SMEM((2, 8), I32),
            pltpu.SMEM((2, 8), I32),
            pltpu.SMEM((2,), I32),
            pltpu.SMEM((8,), F32),
            pltpu.SMEM((8,), F32),
            pltpu.SMEM((8,), F32),
            pltpu.VMEM((1024, 512), BF16),
            pltpu.VMEM((1024, 512), BF16),
            pltpu.VMEM((8, 1024), F32),
            pltpu.VMEM((8, 2, 1024, 256), BF16),
            pltpu.VMEM((1, 512), F32),
            pltpu.VMEM((1024, 256), BF16),
            pltpu.VMEM((64, 64, 256), BF16),
            pltpu.VMEM((8, 128), I32),
            pltpu.VMEM((3, 8, 128), I32),
            pltpu.SMEM((3, 8, 128), I32),
            pltpu.SMEM((3, 16), I32),
            pltpu.VMEM((18, 64, 256), BF16),
            pltpu.VMEM((18, 64, 256), BF16),
            pltpu.VMEM((2, 3, 64, 256), BF16),
            pltpu.VMEM((64, 128), F32),
            pltpu.VMEM((64, 128), F32),
            pltpu.VMEM((64, 128), F32),
            pltpu.VMEM((128, 1024), BF16),
            pltpu.VMEM((8, 128, 512), F32),
            pltpu.VMEM((8, 128, 512), F32),
            pltpu.VMEM((8, 512, 256), F32),
            pltpu.VMEM((8, 128, 256), BF16),
            pltpu.VMEM((2, 512, 256), BF16),
            pltpu.VMEM((128, 128), F32),
            pltpu.VMEM((8, 128), F32),
            pltpu.VMEM((4, 1024, 1024), BF16),
            pltpu.VMEM((4, 256, 1024), BF16),
            pltpu.VMEM((128, 128), F32),
            pltpu.VMEM((2, 4, 3, 2, 128, 512), BF16),
            pltpu.VMEM((2, 4, 2, 128, 512), F32),
            pltpu.VMEM((2, 4, 2, 128, 512), BF16),
            pltpu.VMEM((2, 4, 2, 2, 128, 512), BF16),
            pltpu.VMEM((2, 4, 3, 2, 64, 256), BF16),
            pltpu.VMEM((2, 4, 128, 256), F32),
            pltpu.VMEM((2, 4, 2, 64, 256), BF16),
            pltpu.VMEM((2, 4, 2, 2, 64, 256), BF16),
            pltpu.VMEM((2, 8, 128), F32),
            pltpu.VMEM((8, 128), F32),
            pltpu.VMEM((3, 8, 128), F32),
            pltpu.VMEM((3, 8, 128), F32),
            dma((6,)), dma((8,)), dma((3,)), dma((3,)), dma((3,)), dma((6,)), dma((6,)), dma((6,)),
            dma((4, 4)), dma((4, 4)), dma((4, 4)), dma((4,)), dma((4,)),
            dma((2, 4, 6)), dma((2, 4, 6)), dma((2, 4, 6)), dma((2, 4, 6)),
            dma((7,)), dma((7,)),
        ],
        compiler_params=pltpu.CompilerParams(
            collective_id=0, has_side_effects=True, vmem_limit_bytes=62 * 1024 * 1024
        ),
        cost_estimate=pl.CostEstimate(flops=10000000000, bytes_accessed=24000000, transcendentals=0),
        name="mixer",
    )(owner, slot, spans, decay, bias, skip, x, gate, step, sp, gain, w, res, cache)


def emit_kernel(mixed, state, mixed_out, state_out, sems):
    copies = []
    for i in range(4):
        rows = pl.ds(i * 256, 256)
        copies.append(pltpu.make_async_copy(mixed.at[rows], mixed_out.at[rows], sems.at[i]))
        rows = pl.ds((i % 2) * 256, 256)
        copies.append(pltpu.make_async_copy(state.at[i // 2, rows], state_out.at[i // 2, rows], sems.at[4 + i]))
    for copy in copies:
        copy.start()
    for copy in copies:
        copy.wait()


def emit(mixed, state):
    vmem = pl.BlockSpec(memory_space=pltpu.VMEM)
    hbm = pl.BlockSpec(memory_space=pl.ANY)
    return pl.pallas_call(
        emit_kernel,
        out_shape=(
            jax.ShapeDtypeStruct(mixed.shape, mixed.dtype),
            jax.ShapeDtypeStruct(state.shape, state.dtype),
        ),
        in_specs=[vmem] * 2,
        out_specs=(hbm, hbm),
        scratch_shapes=[pltpu.SemaphoreType.DMA((8,))],
        compiler_params=pltpu.CompilerParams(vmem_limit_bytes=4 * 1024 * 1024),
        name="emit",
    )(mixed, state)


def per_device(
    mixer_input, gate_input, step_raw, state_proj, decay_log, step_bias, skip_gain, norm_gain,
    out_weight, residual, new_spans, hit_owner, hit_slot, state_cache,
):
    mixed, final = mixer(
        hit_owner, hit_slot, new_spans, decay_log, step_bias, skip_gain,
        mixer_input, gate_input, step_raw.T, state_proj.reshape(2, 8192, 256),
        norm_gain.reshape(1, 512), out_weight, residual, state_cache.reshape(64, 64, 256),
    )
    mixed, final = emit(mixed, final)
    return mixed, final.reshape(2, 8, 64, 256)


def solution(mesh):
    in_specs = (
        P("group", "head"),
        P("group", "head"),
        P("group", "head"),
        P(None, "group", None, None),
        P("head"),
        P("head"),
        P("head"),
        P("head"),
        P("head", None),
        P("group", "head"),
        P("group"),
        P("group", "head"),
        P("group", "head"),
        P("group", "head", None, None),
    )
    out_specs = (P("group", "head"), P("group", "head", None, None))
    return jax.shard_map(
        per_device, mesh=mesh, in_specs=in_specs, out_specs=out_specs, check_vma=False
    )
```

```python
import jax
import jax.numpy as jnp
from jax import lax
from jax.experimental import pallas as pl
from jax.experimental.pallas import tpu as pltpu
from jax.sharding import PartitionSpec as P

SPAN = 128
CAP = 6
UNITS = ((2, 1), (2, 0), (3, 1), (3, 0), (1, 1), (0, 1), (1, 0), (0, 0))
SIDE = 4
CHUNKS = 4
WEIGHTS_FIRST = False
BLOCKS = 8
MESH = pl.DeviceIdType.MESH
BF16 = jnp.bfloat16
F32 = jnp.float32
I32 = jnp.int32
HIGHEST = lax.Precision.HIGHEST


def remote(src, dst, send_sem, recv_sem, where):
    return pltpu.make_async_remote_copy(
        src_ref=src, dst_ref=dst, send_sem=send_sem, recv_sem=recv_sem,
        device_id=where, device_id_type=MESH,
    )


def dot_tn(a, b):
    return lax.dot_general(a, b, (((0,), (0,)), ((), ())), preferred_element_type=F32)


def dot_nt(a, b):
    return lax.dot_general(a, b, (((1,), (1,)), ((), ())), preferred_element_type=F32)


def mixer_kernel(
    owner_hbm, slot_hbm, spans_hbm, decay_hbm, bias_hbm, skip_hbm,
    x_hbm, gate_hbm, step_hbm, sp_hbm, gain_hbm, w_hbm, res_hbm, cache_hbm,
    out, h_v,
    owner_s, slot_s, spans_s, decay_s, bias_s, skip_s,
    x_v, gate_v, step_v, sp_v, gain_v, res, cache_v,
    req_v, rreq, req_s, idx_s, pbuf, rbuf, relay,
    e_v, f_v, em_v, sel_v, yi_v, silu_v, ee_v, u_v, c_v, hb_v, ssa, ss_in,
    w_all, g_all, scale_v, s1, own1, r1o, r1n, s2, acc, r2o, r2n,
    ss_mid, ss_core, ss_x, ss_y,
    sem_in, sem_sp, sem_req_s, sem_req_r, sem_rs, sem_st_s, sem_st_r, sem_sc,
    sem_w, sem_ws, sem_wr, sem_gs, sem_gr, sem_1s, sem_1r, sem_2s, sem_2r, sem_ss, sem_sr,
):
    me = lax.axis_index("head")
    deep = lax.axis_index("group")
    core = lax.rem(me, 2)
    col = lax.rem(me // 2, SIDE)
    row = me // (2 * SIDE)

    def head_at(dx, dy, dc):
        y = lax.rem(row + dy, SIDE)
        x = lax.rem(col + dx, SIDE)
        c = lax.rem(core + dc, 2)
        return (y * SIDE + x) * 2 + c

    def at_head(h):
        return {"head": h}

    partner = at_head(head_at(0, 0, 1))
    x_peers = [at_head(head_at(k, 0, 0)) for k in (1, 2, 3)]
    y_peers = [at_head(head_at(0, k, 0)) for k in (1, 2, 3)]
    z_peers = [{"group": lax.rem(deep + k, 4)} for k in (1, 2, 3)]
    p_side = ((x_peers[0], x_peers[2]), (y_peers[0], y_peers[2]))
    q_side = (p_side[1], p_side[0])

    barrier = pltpu.get_barrier_semaphore()
    for peer in z_peers + [partner] + x_peers + y_peers:
        pl.semaphore_signal(barrier, inc=1, device_id=peer, device_id_type=MESH)

    loads = [
        pltpu.make_async_copy(src, dst, sem_in.at[i])
        for i, (src, dst) in enumerate((
            (cache_hbm, cache_v), (step_hbm, step_v), (x_hbm, x_v), (gain_hbm, gain_v),
            (gate_hbm, gate_v), (res_hbm, res),
        ))
    ]

    def sp_copy(b):
        start = pl.multiple_of(b * 1024, 1024)
        return pltpu.make_async_copy(sp_hbm.at[:, pl.ds(start, 1024)], sp_v.at[b], sem_sp.at[b])

    def w_local(dx, dy):
        start = pl.multiple_of(head_at(dx, dy, 0) * 256, 256)
        dst = w_all.at[dx, pl.ds(0, 512), pl.ds(dy * 256, 256)]
        return pltpu.make_async_copy(w_hbm.at[:, pl.ds(start, 256)], dst, sem_w.at[dx, dy])

    def w_remote(dx, dy):
        start = pl.multiple_of(head_at(dx, dy, 1) * 256, 256)
        dst = w_all.at[dx, pl.ds(512, 512), pl.ds(dy * 256, 256)]
        return remote(w_hbm.at[:, pl.ds(start, 256)], dst, sem_ws.at[dx, dy], sem_wr.at[dx, dy], partner)

    def start_weights():
        for dx, dh in UNITS:
            for dy in (2 * dh, 2 * dh + 1):
                w_remote(dx, dy).start()
                w_local(dx, dy).start()
        loads[5].start()

    def g_remote(c):
        return remote(
            g_all.at[c, :, pl.ds(0, 512)], g_all.at[c, :, pl.ds(512, 512)], sem_gs.at[c], sem_gr.at[c], partner
        )

    scalars = [
        pltpu.make_async_copy(src, dst, sem_sc.at[i])
        for i, (src, dst) in enumerate((
            (owner_hbm, owner_s), (slot_hbm, slot_s), (spans_hbm, spans_s),
            (decay_hbm, decay_s), (bias_hbm, bias_s), (skip_hbm, skip_s),
        ))
    ]
    for scalar in scalars:
        scalar.start()
    for load in loads[:5]:
        load.start()
    for b in range(BLOCKS):
        sp_copy(b).start()

    for scalar in scalars:
        scalar.wait()

    lane = lax.broadcasted_iota(I32, (8, 128), 1)
    request = jnp.zeros((8, 128), I32)
    seen = jnp.zeros((8, 128), I32)
    counts = [jnp.int32(0)] * 4
    for e in range(16):
        s, j = divmod(e, 8)
        owner = owner_s[s, j]
        place = slot_s[s, j] * 8 + j
        named = (lane // 8) == owner
        request = jnp.where(jnp.logical_and(named, seen == lane % 8), place, request)
        seen = seen + jnp.where(named, 1, 0)
        rank = jnp.int32(0)
        for q in range(4):
            rank = jnp.where(owner == q, counts[q], rank)
            counts[q] = counts[q] + jnp.where(owner == q, 1, 0)
        away = lax.rem(owner - deep + 4, 4)
        idx_s[0, e] = jnp.where(away == 0, 0, (away - 1) * CAP + jnp.minimum(rank, CAP - 1))
        idx_s[1, e] = jnp.where(away == 0, 1, 0)
        idx_s[2, e] = place
    req_v[...] = request

    def req_copy(k):
        return remote(req_v, rreq.at[k], sem_req_s.at[k], sem_req_r.at[k], z_peers[k])

    pl.semaphore_wait(barrier, 10)
    for k in (0, 2, 1):
        req_copy(k).start()
    if WEIGHTS_FIRST:
        start_weights()

    sub = lax.broadcasted_iota(I32, (8, 128), 0)
    bias = jnp.zeros((8, 128), F32)
    decay = jnp.zeros((8, 128), F32)
    for j in range(8):
        bias = jnp.where(sub == j, bias_s[j], bias)
        decay = jnp.where(sub == j, decay_s[j], decay)
    decay = -jnp.exp(decay)
    loads[1].wait()
    steps = []
    for b in range(BLOCKS):
        raw = step_v[:, b * SPAN:(b + 1) * SPAN] + bias
        alive = jnp.where(b % CHUNKS < spans_s[b // CHUNKS], 1.0, 0.0)
        steps.append((jnp.maximum(raw, 0.0) + jnp.log1p(jnp.exp(-jnp.abs(raw)))) * alive)
    dt = jnp.concatenate(steps, axis=0)
    rate = jnp.concatenate([decay * step for step in steps], axis=0)
    square0 = lax.broadcasted_iota(I32, (SPAN, SPAN), 0)
    square1 = lax.broadcasted_iota(I32, (SPAN, SPAN), 1)
    upper = jnp.where(square0 <= square1, 1.0, 0.0).astype(F32)
    cum = jnp.dot(rate, upper, precision=HIGHEST, preferred_element_type=F32)
    middle = cum[:, SPAN - 1:] * 0.5
    e_v[...] = jnp.exp(cum - middle)
    f_v[...] = jnp.exp(middle - cum) * dt
    em_v[...] = jnp.exp(jnp.broadcast_to(middle, (BLOCKS * 8, 128)))
    ssa[...] = jnp.zeros((SPAN, SPAN), F32)

    def state_copy(i):
        src, dst, way = (
            (pbuf.at[pl.ds(6, 3)], rbuf.at[pl.ds(6, 3)], 1),
            (pbuf.at[pl.ds(9, 3)], rbuf.at[pl.ds(9, 3)], 1),
            (pbuf.at[pl.ds(0, 6)], rbuf.at[pl.ds(0, 6)], 2),
            (pbuf.at[pl.ds(12, 6)], rbuf.at[pl.ds(12, 6)], 0),
        )[i]
        return remote(src, dst, sem_st_s.at[i], sem_st_r.at[i], z_peers[way])

    loads[0].wait()
    for k in (0, 2, 1):
        req_copy(k).wait_recv()
        list_k = rreq[k]
        for r in range(CAP):
            place = jnp.sum(jnp.where(lane[:1] == deep * 8 + r, list_k[:1], 0))
            pbuf[k * CAP + r] = cache_v[place]
            if k == 1 and r == 2:
                state_copy(0).start()
        state_copy((2, 1, 3)[k]).start()
    if not WEIGHTS_FIRST:
        start_weights()

    pick = me // 4
    sel_v[...] = jnp.where(
        lax.broadcasted_iota(I32, (SPAN, 1024), 1) == lax.broadcasted_iota(I32, (SPAN, 1024), 0) * 8 + pick, 1.0, 0.0
    ).astype(BF16)
    channel = lax.broadcasted_iota(I32, (16, 512), 1)
    spread = jnp.where(channel // 64 == lax.broadcasted_iota(I32, (16, 512), 0) % 8, 1.0, 0.0).astype(BF16)
    channel = lax.broadcasted_iota(I32, (1, 512), 1)
    skip = jnp.zeros((1, 512), F32)
    for j in range(8):
        skip = jnp.where(channel // 64 == j, skip_s[j], skip)
    for load in loads[2:5]:
        load.wait()

    def widen(part):
        high = part.astype(BF16)
        low = (part - high.astype(F32)).astype(BF16)
        return dot_tn(jnp.concatenate([high, low], axis=0), spread)

    def prepare(b, _):
        sp_copy(b).wait()
        few = pl.ds(pl.multiple_of(b * 8, 8), 8)
        x = x_v[pl.ds(pl.multiple_of(b * SPAN, SPAN), SPAN), :].astype(F32)
        wide_e = widen(e_v[few, :])
        ee_v[b] = wide_e
        z = (widen(f_v[few, :]) * x).astype(BF16)
        b_rows = jnp.dot(sel_v[...], sp_v[b, 0], preferred_element_type=F32).astype(BF16)
        c_rows = jnp.dot(sel_v[...], sp_v[b, 1], preferred_element_type=F32).astype(BF16)
        c_v[b] = c_rows
        scores = jnp.where(square0 >= square1, dot_nt(c_rows, b_rows), 0.0).astype(BF16)
        yi_v[b] = wide_e * jnp.dot(scores, z, preferred_element_type=F32) + skip * x
        u_v[b] = dot_tn(z, b_rows)
        gate = gate_v[pl.ds(pl.multiple_of(b * SPAN, SPAN), SPAN), :].astype(F32)
        silu_v[b] = gate / (1.0 + jnp.exp(-gate))
        return 0

    lax.fori_loop(0, BLOCKS, prepare, 0)

    for i in (0, 1, 2, 3):
        state_copy(i).wait_recv()
    for e in range(16):
        s, j = divmod(e, 8)
        here = cache_v[idx_s[2, e]].astype(F32)
        sent = rbuf[idx_s[0, e]].astype(F32)
        h_v[s, j * 64:(j + 1) * 64, :] = jnp.where(idx_s[1, e] == 1, here, sent)

    def fade_of(b, j):
        fade = em_v[pl.ds(b * 8 + j, 1), :]
        return jnp.concatenate([fade, fade], axis=1)

    def stage_states(c):
        for s in (0, 1):
            b = s * CHUNKS + c
            for j in range(8):
                rows = slice(j * 64, (j + 1) * 64)
                hb_v[s, rows, :] = (h_v[s, rows, :] * fade_of(b, j)).astype(BF16)
            y = yi_v[b] + ee_v[b] * dot_nt(c_v[b], hb_v[s])
            gated = y * silu_v[b]
            g_all[c, s * SPAN:(s + 1) * SPAN, :512] = (gated * gain_v[...]).astype(BF16)
            yi_v[b] = gated
        g_remote(c).start()
        for s in (0, 1):
            b = s * CHUNKS + c
            gated = yi_v[b]
            ssa[...] = jnp.where(square1 == b, jnp.sum(gated * gated, axis=1, keepdims=True), ssa[...])
            for j in range(8):
                rows = slice(j * 64, (j + 1) * 64)
                fade = fade_of(b, j)
                h_v[s, rows, :] = (h_v[s, rows, :] * fade + u_v[b, rows, :]) * fade


    def ss_core_copy():
        return remote(ss_in, ss_core, sem_ss.at[0], sem_sr.at[0], partner)

    def ss_x_copy(k):
        return remote(ss_mid.at[0], ss_x.at[k], sem_ss.at[1 + k], sem_sr.at[1 + k], x_peers[k])

    def ss_y_copy(k):
        return remote(ss_mid.at[1], ss_y.at[k], sem_ss.at[4 + k], sem_sr.at[4 + k], y_peers[k])

    def first(part, c, kind):
        if kind == 0:
            src, dst, way = s1.at[part, c, 1, 0], r1o.at[part, c, 0], 0
        elif kind == 1:
            src, dst, way = s1.at[part, c, 1, 1], r1o.at[part, c, 1], 1
        elif kind == 2:
            src, dst, way = s1.at[part, c, 0, 1], r1n.at[part, c, 0, 1], 0
        elif kind == 3:
            src, dst, way = s1.at[part, c, 2, 0], r1n.at[part, c, 1, 0], 1
        elif kind == 4:
            src, dst, way = s1.at[part, c, 0, 0], r1n.at[part, c, 0, 0], 0
        else:
            src, dst, way = s1.at[part, c, 2, 1], r1n.at[part, c, 1, 1], 1
        return remote(src, dst, sem_1s.at[part, c, kind], sem_1r.at[part, c, kind], p_side[part][way])

    def second_to(part, c, way):
        if way < 2:
            return q_side[part][way]
        near = q_side[part][way - 2]["head"]
        far = (y_peers, x_peers)[part][1]["head"]
        return at_head(jnp.where(c == CHUNKS - 1, far, near))

    def second(part, c, kind):
        if kind == 0:
            src, dst, way = s2.at[part, c, 1, 0], r2o.at[part, c, 0], 2
        elif kind == 1:
            src, dst, way = s2.at[part, c, 1, 1], r2o.at[part, c, 1], 3
        elif kind == 2:
            src, dst, way = s2.at[part, c, 0, 1], r2n.at[part, c, 0, 1], 0
        elif kind == 3:
            src, dst, way = s2.at[part, c, 2, 0], r2n.at[part, c, 1, 0], 1
        elif kind == 4:
            src, dst, way = s2.at[part, c, 0, 0], r2n.at[part, c, 0, 0], 0
        else:
            src, dst, way = s2.at[part, c, 2, 1], r2n.at[part, c, 1, 1], 1
        return remote(src, dst, sem_2s.at[part, c, kind], sem_2r.at[part, c, kind], second_to(part, c, way))

    IMMEDIATE = {(2, 0): 0, (2, 1): 1, (1, 1): 2, (3, 0): 3}

    def stage_project(c):
        g_remote(c).wait_recv()
        done = set()
        for dx, dh in UNITS:
            @pl.when(c == 0)
            def _():
                for dy in (2 * dh, 2 * dh + 1):
                    w_local(dx, dy).wait()
                    w_remote(dx, dy).wait_recv()
            term = jnp.dot(g_all[c], w_all[dx, :, dh * 512:(dh + 1) * 512], preferred_element_type=F32)
            for dy in (2 * dh, 2 * dh + 1):
                for part, dp, dq in ((0, dx, dy), (1, dy, dx)):
                    piece = term[part * SPAN:(part + 1) * SPAN, (dy % 2) * 256:(dy % 2 + 1) * 256]
                    columns = pl.ds((dq % 2) * 256, 256)
                    if dp == 0:
                        own1[part, c, dq // 2, :, columns] = piece
                    else:
                        s1[part, c, dp - 1, dq // 2, :, columns] = piece.astype(BF16)
            for dy in (2 * dh, 2 * dh + 1):
                for part, dp, dq in ((0, dx, dy), (1, dy, dx)):
                    done.add((part, dp, dq))
                    kind = IMMEDIATE.get((dp, dq // 2))
                    if kind is not None and (part, dp, dq ^ 1) in done:
                        first(part, c, kind).start()

    def stage_pass1(c):
        for part in (0, 1):
            for way, (dp, half) in enumerate(((0, 0), (2, 1))):
                first(part, c, way).wait_recv()
                total = s1[part, c, dp, half].astype(F32) + r1o[part, c, way].astype(F32)
                s1[part, c, dp, half] = total.astype(BF16)
                first(part, c, 4 + way).start()

    def stage_turn(c):
        for part in (0, 1):
            first(part, c, 2).wait_recv()
            first(part, c, 5).wait_recv()
            total = own1[part, c, 1] + r1n[part, c, 0, 1].astype(F32) + r1n[part, c, 1, 1].astype(F32)
            s2[part, c, 1, 0] = total[:64, :256].astype(BF16)
            second(part, c, 0).start()
            s2[part, c, 1, 1] = total[64:, :256].astype(BF16)
            second(part, c, 1).start()
            s2[part, c, 2, 0] = total[:64, 256:].astype(BF16)
            second(part, c, 3).start()
            s2[part, c, 2, 1] = total[64:, 256:].astype(BF16)
        for part in (0, 1):
            first(part, c, 4).wait_recv()
            first(part, c, 3).wait_recv()
            total = own1[part, c, 0] + r1n[part, c, 0, 0].astype(F32) + r1n[part, c, 1, 0].astype(F32)
            s2[part, c, 0, 1] = total[64:, 256:].astype(BF16)
            second(part, c, 2).start()
            s2[part, c, 0, 0] = total[:64, 256:].astype(BF16)
            acc[part, c] = total[:, :256]

        @pl.when(c == CHUNKS - 1)
        def _():
            for part in (0, 1):
                second(part, c, 4).start()
                second(part, c, 5).start()

    def stage_pass2(c):
        @pl.when(c < CHUNKS - 1)
        def _():
            for part in (0, 1):
                for way, (dp, half) in enumerate(((0, 0), (2, 1))):
                    second(part, c, way).wait_recv()
                    total = s2[part, c, dp, half].astype(F32) + r2o[part, c, way].astype(F32)
                    s2[part, c, dp, half] = total.astype(BF16)
                    second(part, c, 4 + way).start()

    def stage_last(c):
        @pl.when(c == CHUNKS - 1)
        def _():
            for part in (0, 1):
                for half in (0, 1):
                    second(part, c, half).wait_recv()
                    acc[part, c, pl.ds(half * 64, 64)] += r2o[part, c, half].astype(F32)

        for part in (0, 1):
            for half in (0, 1):
                second(part, c, 2 if half else 4).wait_recv()
                second(part, c, 5 if half else 3).wait_recv()
                acc[part, c, pl.ds(half * 64, 64)] += (
                    r2n[part, c, 0, half].astype(F32) + r2n[part, c, 1, half].astype(F32)
                )

    def finish(c):
        for part in (0, 1):
            b = part * CHUNKS + c
            rows = pl.ds(pl.multiple_of(b * SPAN, SPAN), SPAN)
            scale = jnp.sum(jnp.where(square1 == b, scale_v[...], 0.0), axis=1, keepdims=True)
            out[rows, :] = (res[rows, :].astype(F32) + acc[part, c] * scale).astype(BF16)

    def drain_first(c):
        for part in (0, 1):
            for kind in range(6):
                first(part, c, kind).wait_send()
        g_remote(c).wait_send()

    def drain_second(c):
        @pl.when(c < CHUNKS - 1)
        def _():
            for part in (0, 1):
                for kind in range(6):
                    second(part, c, kind).wait_send()

    def drain_rest():
        for dx, dh in UNITS:
            for dy in (2 * dh, 2 * dh + 1):
                w_remote(dx, dy).wait_send()
        for k in range(3):
            req_copy(k).wait_send()
        for i in range(4):
            state_copy(i).wait_send()

    def step(t, _):
        @pl.when(t < CHUNKS - 1)
        def _():
            stage_states(t + 1)

        @pl.when(t < CHUNKS)
        def _():
            stage_project(t)

        @pl.when(t == 2)
        def _():
            ss_in[...] = jnp.transpose(ssa[...])[:8]
            ss_core_copy().start()

        @pl.when(t == 3)
        def _():
            ss_core_copy().wait()
            ss_mid[0] = ss_in[...] + ss_core[...]
            for k in range(3):
                ss_x_copy(k).start()

        @pl.when(t == 4)
        def _():
            for k in range(3):
                ss_x_copy(k).wait()
            ss_mid[1] = ss_mid[0] + ss_x[0] + ss_x[1] + ss_x[2]
            for k in range(3):
                ss_y_copy(k).start()

        @pl.when(t == 4)
        def _():
            drain_rest()

        for lag, stage in ((2, stage_pass1), (3, stage_turn), (4, stage_pass2), (5, stage_last), (5, drain_first), (6, drain_second)):
            @pl.when(jnp.logical_and(t >= lag, t < CHUNKS + lag))
            def _():
                stage(t - lag)

        @pl.when(t == 6)
        def _():
            for k in range(3):
                ss_y_copy(k).wait()
            loads[5].wait()
            total = ss_mid[1] + ss_y[0] + ss_y[1] + ss_y[2]
            scale = lax.rsqrt(total / 16384.0 + 1e-05)
            scale_v[...] = jnp.transpose(jnp.concatenate([scale] * 16, axis=0))
            finish(0)

        @pl.when(t >= 6)
        def _():
            finish(t - 5)
        return 0

    stage_states(0)
    lax.fori_loop(0, CHUNKS + 5, step, 0)

    for part in (0, 1):
        for kind in range(6):
            second(part, CHUNKS - 1, kind).wait_send()


def mixer(owner, slot, spans, decay, bias, skip, x, gate, step, sp, gain, w, res, cache):
    vmem = pl.BlockSpec(memory_space=pltpu.VMEM)
    hbm = pl.BlockSpec(memory_space=pl.ANY)
    dma = pltpu.SemaphoreType.DMA
    return pl.pallas_call(
        mixer_kernel,
        out_shape=(
            pltpu.VMEM(res.shape, res.dtype),
            pltpu.VMEM((2, 512, 256), F32),
        ),
        in_specs=[hbm] * 14,
        out_specs=(vmem, vmem),
        scratch_shapes=[
            pltpu.SMEM((2, 8), I32),
            pltpu.SMEM((2, 8), I32),
            pltpu.SMEM((2,), I32),
            pltpu.SMEM((8,), F32),
            pltpu.SMEM((8,), F32),
            pltpu.SMEM((8,), F32),
            pltpu.VMEM((1024, 512), BF16),
            pltpu.VMEM((1024, 512), BF16),
            pltpu.VMEM((8, 1024), F32),
            pltpu.VMEM((8, 2, 1024, 256), BF16),
            pltpu.VMEM((1, 512), F32),
            pltpu.VMEM((1024, 256), BF16),
            pltpu.VMEM((64, 64, 256), BF16),
            pltpu.VMEM((8, 128), I32),
            pltpu.VMEM((3, 8, 128), I32),
            pltpu.SMEM((3, 8, 128), I32),
            pltpu.SMEM((3, 16), I32),
            pltpu.VMEM((18, 64, 256), BF16),
            pltpu.VMEM((18, 64, 256), BF16),
            pltpu.VMEM((2, 3, 64, 256), BF16),
            pltpu.VMEM((64, 128), F32),
            pltpu.VMEM((64, 128), F32),
            pltpu.VMEM((64, 128), F32),
            pltpu.VMEM((128, 1024), BF16),
            pltpu.VMEM((8, 128, 512), F32),
            pltpu.VMEM((8, 128, 512), F32),
            pltpu.VMEM((8, 128, 512), F32),
            pltpu.VMEM((8, 512, 256), F32),
            pltpu.VMEM((8, 128, 256), BF16),
            pltpu.VMEM((2, 512, 256), BF16),
            pltpu.VMEM((128, 128), F32),
            pltpu.VMEM((8, 128), F32),
            pltpu.VMEM((4, 1024, 1024), BF16),
            pltpu.VMEM((4, 256, 1024), BF16),
            pltpu.VMEM((128, 128), F32),
            pltpu.VMEM((2, 4, 3, 2, 128, 512), BF16),
            pltpu.VMEM((2, 4, 2, 128, 512), F32),
            pltpu.VMEM((2, 4, 2, 128, 512), BF16),
            pltpu.VMEM((2, 4, 2, 2, 128, 512), BF16),
            pltpu.VMEM((2, 4, 3, 2, 64, 256), BF16),
            pltpu.VMEM((2, 4, 128, 256), F32),
            pltpu.VMEM((2, 4, 2, 64, 256), BF16),
            pltpu.VMEM((2, 4, 2, 2, 64, 256), BF16),
            pltpu.VMEM((2, 8, 128), F32),
            pltpu.VMEM((8, 128), F32),
            pltpu.VMEM((3, 8, 128), F32),
            pltpu.VMEM((3, 8, 128), F32),
            dma((6,)), dma((8,)), dma((3,)), dma((3,)), dma((3,)), dma((4,)), dma((4,)), dma((6,)),
            dma((4, 4)), dma((4, 4)), dma((4, 4)), dma((4,)), dma((4,)),
            dma((2, 4, 6)), dma((2, 4, 6)), dma((2, 4, 6)), dma((2, 4, 6)),
            dma((7,)), dma((7,)),
        ],
        compiler_params=pltpu.CompilerParams(
            collective_id=0, has_side_effects=True, vmem_limit_bytes=61 * 1024 * 1024
        ),
        cost_estimate=pl.CostEstimate(flops=10000000000, bytes_accessed=24000000, transcendentals=0),
        name="mixer",
    )(owner, slot, spans, decay, bias, skip, x, gate, step, sp, gain, w, res, cache)


def emit_kernel(mixed, state, mixed_out, state_out, sems):
    copies = []
    for i in range(4):
        rows = pl.ds(i * 256, 256)
        copies.append(pltpu.make_async_copy(mixed.at[rows], mixed_out.at[rows], sems.at[i]))
        rows = pl.ds((i % 2) * 256, 256)
        copies.append(pltpu.make_async_copy(state.at[i // 2, rows], state_out.at[i // 2, rows], sems.at[4 + i]))
    for copy in copies:
        copy.start()
    for copy in copies:
        copy.wait()


def emit(mixed, state):
    vmem = pl.BlockSpec(memory_space=pltpu.VMEM)
    hbm = pl.BlockSpec(memory_space=pl.ANY)
    return pl.pallas_call(
        emit_kernel,
        out_shape=(
            jax.ShapeDtypeStruct(mixed.shape, mixed.dtype),
            jax.ShapeDtypeStruct(state.shape, state.dtype),
        ),
        in_specs=[vmem] * 2,
        out_specs=(hbm, hbm),
        scratch_shapes=[pltpu.SemaphoreType.DMA((8,))],
        compiler_params=pltpu.CompilerParams(vmem_limit_bytes=4 * 1024 * 1024),
        name="emit",
    )(mixed, state)


def per_device(
    mixer_input, gate_input, step_raw, state_proj, decay_log, step_bias, skip_gain, norm_gain,
    out_weight, residual, new_spans, hit_owner, hit_slot, state_cache,
):
    mixed, final = mixer(
        hit_owner, hit_slot, new_spans, decay_log, step_bias, skip_gain,
        mixer_input, gate_input, step_raw.T, state_proj.reshape(2, 8192, 256),
        norm_gain.reshape(1, 512), out_weight, residual, state_cache.reshape(64, 64, 256),
    )
    mixed, final = emit(mixed, final)
    return mixed, final.reshape(2, 8, 64, 256)


def solution(mesh):
    in_specs = (
        P("group", "head"),
        P("group", "head"),
        P("group", "head"),
        P(None, "group", None, None),
        P("head"),
        P("head"),
        P("head"),
        P("head"),
        P("head", None),
        P("group", "head"),
        P("group"),
        P("group", "head"),
        P("group", "head"),
        P("group", "head", None, None),
    )
    out_specs = (P("group", "head"), P("group", "head", None, None))
    return jax.shard_map(
        per_device, mesh=mesh, in_specs=in_specs, out_specs=out_specs, check_vma=False
    )
```

```python
import jax
import jax.numpy as jnp
from jax import lax
from jax.experimental import pallas as pl
from jax.experimental.pallas import tpu as pltpu
from jax.sharding import PartitionSpec as P

SPAN = 128
CAP = 6
UNITS = ((2, 1), (2, 0), (3, 1), (3, 0), (1, 1), (0, 1), (1, 0), (0, 0))
SIDE = 4
CHUNKS = 4
WEIGHTS_FIRST = False
BLOCKS = 8
MESH = pl.DeviceIdType.MESH
BF16 = jnp.bfloat16
F32 = jnp.float32
I32 = jnp.int32
HIGHEST = lax.Precision.HIGHEST


def remote(src, dst, send_sem, recv_sem, where):
    return pltpu.make_async_remote_copy(
        src_ref=src, dst_ref=dst, send_sem=send_sem, recv_sem=recv_sem,
        device_id=where, device_id_type=MESH,
    )


def dot_tn(a, b):
    return lax.dot_general(a, b, (((0,), (0,)), ((), ())), preferred_element_type=F32)


def dot_nt(a, b):
    return lax.dot_general(a, b, (((1,), (1,)), ((), ())), preferred_element_type=F32)


def mixer_kernel(
    owner_hbm, slot_hbm, spans_hbm, decay_hbm, bias_hbm, skip_hbm,
    x_hbm, gate_hbm, step_hbm, sp_hbm, gain_hbm, w_hbm, res_hbm, cache_hbm,
    out, h_v,
    owner_s, slot_s, spans_s, decay_s, bias_s, skip_s,
    x_v, gate_v, step_v, sp_v, gain_v, res, cache_v,
    req_v, rreq, req_s, idx_s, pbuf, rbuf, relay,
    e_v, f_v, em_v, sel_v, yi_v, silu_v, ee_v, u_v, c_v, hb_v, ssa, ss_in,
    w_all, g_all, scale_v, s1, own1, r1o, r1n, s2, acc, r2o, r2n,
    ss_mid, ss_core, ss_x, ss_y,
    sem_in, sem_sp, sem_req_s, sem_req_r, sem_rs, sem_st_s, sem_st_r, sem_sc,
    sem_w, sem_ws, sem_wr, sem_gs, sem_gr, sem_1s, sem_1r, sem_2s, sem_2r, sem_ss, sem_sr,
):
    me = lax.axis_index("head")
    deep = lax.axis_index("group")
    core = lax.rem(me, 2)
    col = lax.rem(me // 2, SIDE)
    row = me // (2 * SIDE)

    def head_at(dx, dy, dc):
        y = lax.rem(row + dy, SIDE)
        x = lax.rem(col + dx, SIDE)
        c = lax.rem(core + dc, 2)
        return (y * SIDE + x) * 2 + c

    def at_head(h):
        return {"head": h}

    partner = at_head(head_at(0, 0, 1))
    x_peers = [at_head(head_at(k, 0, 0)) for k in (1, 2, 3)]
    y_peers = [at_head(head_at(0, k, 0)) for k in (1, 2, 3)]
    z_peers = [{"group": lax.rem(deep + k, 4)} for k in (1, 2, 3)]
    p_side = ((x_peers[0], x_peers[2]), (y_peers[0], y_peers[2]))
    q_side = (p_side[1], p_side[0])

    barrier = pltpu.get_barrier_semaphore()
    for peer in z_peers + [partner] + x_peers + y_peers:
        pl.semaphore_signal(barrier, inc=1, device_id=peer, device_id_type=MESH)

    loads = [
        pltpu.make_async_copy(src, dst, sem_in.at[i])
        for i, (src, dst) in enumerate((
            (cache_hbm, cache_v), (step_hbm, step_v), (x_hbm, x_v), (gain_hbm, gain_v),
            (gate_hbm, gate_v), (res_hbm, res),
        ))
    ]

    def sp_copy(b):
        start = pl.multiple_of(b * 1024, 1024)
        return pltpu.make_async_copy(sp_hbm.at[:, pl.ds(start, 1024)], sp_v.at[b], sem_sp.at[b])

    def w_local(dx, dy):
        start = pl.multiple_of(head_at(dx, dy, 0) * 256, 256)
        dst = w_all.at[dx, pl.ds(0, 512), pl.ds(dy * 256, 256)]
        return pltpu.make_async_copy(w_hbm.at[:, pl.ds(start, 256)], dst, sem_w.at[dx, dy])

    def w_remote(dx, dy):
        start = pl.multiple_of(head_at(dx, dy, 1) * 256, 256)
        dst = w_all.at[dx, pl.ds(512, 512), pl.ds(dy * 256, 256)]
        return remote(w_hbm.at[:, pl.ds(start, 256)], dst, sem_ws.at[dx, dy], sem_wr.at[dx, dy], partner)

    def start_weights():
        for dx, dh in UNITS:
            for dy in (2 * dh, 2 * dh + 1):
                w_remote(dx, dy).start()
                w_local(dx, dy).start()
        loads[5].start()

    def g_remote(c):
        return remote(
            g_all.at[c, :, pl.ds(0, 512)], g_all.at[c, :, pl.ds(512, 512)], sem_gs.at[c], sem_gr.at[c], partner
        )

    scalars = [
        pltpu.make_async_copy(src, dst, sem_sc.at[i])
        for i, (src, dst) in enumerate((
            (owner_hbm, owner_s), (slot_hbm, slot_s), (spans_hbm, spans_s),
            (decay_hbm, decay_s), (bias_hbm, bias_s), (skip_hbm, skip_s),
        ))
    ]
    for scalar in scalars:
        scalar.start()
    for load in loads[:5]:
        load.start()
    for b in range(BLOCKS):
        sp_copy(b).start()

    for scalar in scalars[:2]:
        scalar.wait()

    lane = lax.broadcasted_iota(I32, (8, 128), 1)
    lane_owner = lane // 8
    lane_rank = lane % 8
    request = jnp.zeros((8, 128), I32)
    for e in range(16):
        s, j = divmod(e, 8)
        named = lane_owner == owner_s[s, j]
        request = jnp.where(jnp.logical_and(named, lane_rank == 0), slot_s[s, j] * 8 + j, request)
        lane_rank = lane_rank - jnp.where(named, 1, 0)
    req_v[...] = request

    def req_copy(k):
        return remote(req_v, rreq.at[k], sem_req_s.at[k], sem_req_r.at[k], z_peers[k])

    pl.semaphore_wait(barrier, 10)
    for k in (0, 2, 1):
        req_copy(k).start()
    if WEIGHTS_FIRST:
        start_weights()

    for scalar in scalars[2:]:
        scalar.wait()

    sub = lax.broadcasted_iota(I32, (8, 128), 0)
    bias = jnp.zeros((8, 128), F32)
    decay = jnp.zeros((8, 128), F32)
    for j in range(8):
        bias = jnp.where(sub == j, bias_s[j], bias)
        decay = jnp.where(sub == j, decay_s[j], decay)
    decay = -jnp.exp(decay)
    loads[1].wait()
    steps = []
    for b in range(BLOCKS):
        raw = step_v[:, b * SPAN:(b + 1) * SPAN] + bias
        alive = jnp.where(b % CHUNKS < spans_s[b // CHUNKS], 1.0, 0.0)
        steps.append((jnp.maximum(raw, 0.0) + jnp.log1p(jnp.exp(-jnp.abs(raw)))) * alive)
    dt = jnp.concatenate(steps, axis=0)
    rate = jnp.concatenate([decay * step for step in steps], axis=0)
    square0 = lax.broadcasted_iota(I32, (SPAN, SPAN), 0)
    square1 = lax.broadcasted_iota(I32, (SPAN, SPAN), 1)
    upper = jnp.where(square0 <= square1, 1.0, 0.0).astype(F32)
    cum = jnp.dot(rate, upper, precision=HIGHEST, preferred_element_type=F32)
    middle = cum[:, SPAN - 1:] * 0.5
    e_v[...] = jnp.exp(cum - middle)
    f_v[...] = jnp.exp(middle - cum) * dt
    em_v[...] = jnp.exp(jnp.broadcast_to(middle, (BLOCKS * 8, 128)))
    ssa[...] = jnp.zeros((SPAN, SPAN), F32)

    def state_copy(i):
        src, dst, way = (
            (pbuf.at[pl.ds(6, 3)], rbuf.at[pl.ds(6, 3)], 1),
            (pbuf.at[pl.ds(9, 3)], rbuf.at[pl.ds(9, 3)], 1),
            (pbuf.at[pl.ds(0, 6)], rbuf.at[pl.ds(0, 6)], 2),
            (pbuf.at[pl.ds(12, 6)], rbuf.at[pl.ds(12, 6)], 0),
        )[i]
        return remote(src, dst, sem_st_s.at[i], sem_st_r.at[i], z_peers[way])

    loads[0].wait()
    for k in (0, 2, 1):
        req_copy(k).wait_recv()
        list_k = rreq[k]
        for r in range(CAP):
            place = jnp.sum(jnp.where(lane[:1] == deep * 8 + r, list_k[:1], 0))
            pbuf[k * CAP + r] = cache_v[place]
            if k == 1 and r == 2:
                state_copy(0).start()
        state_copy((2, 1, 3)[k]).start()
    if not WEIGHTS_FIRST:
        start_weights()

    counts = [jnp.int32(0)] * 4
    for e in range(16):
        s, j = divmod(e, 8)
        owner = owner_s[s, j]
        rank = jnp.int32(0)
        for q in range(4):
            rank = jnp.where(owner == q, counts[q], rank)
            counts[q] = counts[q] + jnp.where(owner == q, 1, 0)
        away = lax.rem(owner - deep + 4, 4)
        idx_s[0, e] = jnp.where(away == 0, 0, (away - 1) * CAP + jnp.minimum(rank, CAP - 1))
        idx_s[1, e] = jnp.where(away == 0, 1, 0)
        idx_s[2, e] = slot_s[s, j] * 8 + j

    pick = me // 4
    sel_v[...] = jnp.where(
        lax.broadcasted_iota(I32, (SPAN, 1024), 1) == lax.broadcasted_iota(I32, (SPAN, 1024), 0) * 8 + pick, 1.0, 0.0
    ).astype(BF16)
    channel = lax.broadcasted_iota(I32, (16, 512), 1)
    spread = jnp.where(channel // 64 == lax.broadcasted_iota(I32, (16, 512), 0) % 8, 1.0, 0.0).astype(BF16)
    channel = lax.broadcasted_iota(I32, (1, 512), 1)
    skip = jnp.zeros((1, 512), F32)
    for j in range(8):
        skip = jnp.where(channel // 64 == j, skip_s[j], skip)
    for load in loads[2:5]:
        load.wait()

    def widen(part):
        high = part.astype(BF16)
        low = (part - high.astype(F32)).astype(BF16)
        return dot_tn(jnp.concatenate([high, low], axis=0), spread)

    def prepare(b, _):
        sp_copy(b).wait()
        few = pl.ds(pl.multiple_of(b * 8, 8), 8)
        x = x_v[pl.ds(pl.multiple_of(b * SPAN, SPAN), SPAN), :].astype(F32)
        wide_e = widen(e_v[few, :])
        ee_v[b] = wide_e
        z = (widen(f_v[few, :]) * x).astype(BF16)
        b_rows = jnp.dot(sel_v[...], sp_v[b, 0], preferred_element_type=F32).astype(BF16)
        c_rows = jnp.dot(sel_v[...], sp_v[b, 1], preferred_element_type=F32).astype(BF16)
        c_v[b] = c_rows
        scores = jnp.where(square0 >= square1, dot_nt(c_rows, b_rows), 0.0).astype(BF16)
        yi_v[b] = wide_e * jnp.dot(scores, z, preferred_element_type=F32) + skip * x
        u_v[b] = dot_tn(z, b_rows)
        gate = gate_v[pl.ds(pl.multiple_of(b * SPAN, SPAN), SPAN), :].astype(F32)
        silu_v[b] = gate / (1.0 + jnp.exp(-gate))
        return 0

    lax.fori_loop(0, BLOCKS, prepare, 0)

    def fade_of(b, j):
        fade = em_v[pl.ds(b * 8 + j, 1), :]
        return jnp.concatenate([fade, fade], axis=1)

    for i in (0, 1, 2, 3):
        state_copy(i).wait_recv()
    for e in range(16):
        s, j = divmod(e, 8)
        here = cache_v[idx_s[2, e]].astype(F32)
        sent = rbuf[idx_s[0, e]].astype(F32)
        state = jnp.where(idx_s[1, e] == 1, here, sent)
        rows = slice(j * 64, (j + 1) * 64)
        h_v[s, rows, :] = state
        hb_v[s, rows, :] = (state * fade_of(s * CHUNKS, j)).astype(BF16)

    def stage_states(c, fresh=False):
        for s in (0, 1):
            b = s * CHUNKS + c
            for j in range(0 if fresh else 8):
                rows = slice(j * 64, (j + 1) * 64)
                hb_v[s, rows, :] = (h_v[s, rows, :] * fade_of(b, j)).astype(BF16)
            y = yi_v[b] + ee_v[b] * dot_nt(c_v[b], hb_v[s])
            gated = y * silu_v[b]
            g_all[c, s * SPAN:(s + 1) * SPAN, :512] = (gated * gain_v[...]).astype(BF16)
            yi_v[b] = gated
        g_remote(c).start()
        for s in (0, 1):
            b = s * CHUNKS + c
            gated = yi_v[b]
            ssa[...] = jnp.where(square1 == b, jnp.sum(gated * gated, axis=1, keepdims=True), ssa[...])
            for j in range(8):
                rows = slice(j * 64, (j + 1) * 64)
                fade = fade_of(b, j)
                h_v[s, rows, :] = (h_v[s, rows, :] * fade + u_v[b, rows, :]) * fade


    def ss_core_copy():
        return remote(ss_in, ss_core, sem_ss.at[0], sem_sr.at[0], partner)

    def ss_x_copy(k):
        return remote(ss_mid.at[0], ss_x.at[k], sem_ss.at[1 + k], sem_sr.at[1 + k], x_peers[k])

    def ss_y_copy(k):
        return remote(ss_mid.at[1], ss_y.at[k], sem_ss.at[4 + k], sem_sr.at[4 + k], y_peers[k])

    def first(part, c, kind):
        if kind == 0:
            src, dst, way = s1.at[part, c, 1, 0], r1o.at[part, c, 0], 0
        elif kind == 1:
            src, dst, way = s1.at[part, c, 1, 1], r1o.at[part, c, 1], 1
        elif kind == 2:
            src, dst, way = s1.at[part, c, 0, 1], r1n.at[part, c, 0, 1], 0
        elif kind == 3:
            src, dst, way = s1.at[part, c, 2, 0], r1n.at[part, c, 1, 0], 1
        elif kind == 4:
            src, dst, way = s1.at[part, c, 0, 0], r1n.at[part, c, 0, 0], 0
        else:
            src, dst, way = s1.at[part, c, 2, 1], r1n.at[part, c, 1, 1], 1
        return remote(src, dst, sem_1s.at[part, c, kind], sem_1r.at[part, c, kind], p_side[part][way])

    def second_to(part, c, way):
        if way < 2:
            return q_side[part][way]
        near = q_side[part][way - 2]["head"]
        far = (y_peers, x_peers)[part][1]["head"]
        return at_head(jnp.where(c == CHUNKS - 1, far, near))

    def second(part, c, kind):
        if kind == 0:
            src, dst, way = s2.at[part, c, 1, 0], r2o.at[part, c, 0], 2
        elif kind == 1:
            src, dst, way = s2.at[part, c, 1, 1], r2o.at[part, c, 1], 3
        elif kind == 2:
            src, dst, way = s2.at[part, c, 0, 1], r2n.at[part, c, 0, 1], 0
        elif kind == 3:
            src, dst, way = s2.at[part, c, 2, 0], r2n.at[part, c, 1, 0], 1
        elif kind == 4:
            src, dst, way = s2.at[part, c, 0, 0], r2n.at[part, c, 0, 0], 0
        else:
            src, dst, way = s2.at[part, c, 2, 1], r2n.at[part, c, 1, 1], 1
        return remote(src, dst, sem_2s.at[part, c, kind], sem_2r.at[part, c, kind], second_to(part, c, way))

    IMMEDIATE = {(2, 0): 0, (2, 1): 1, (1, 1): 2, (3, 0): 3}

    def stage_pass1(c):
        for part in (0, 1):
            for way, (dp, half) in enumerate(((0, 0), (2, 1))):
                first(part, c, way).wait_recv()
                total = s1[part, c, dp, half].astype(F32) + r1o[part, c, way].astype(F32)
                s1[part, c, dp, half] = total.astype(BF16)
                first(part, c, 4 + way).start()

    def stage_project(c):
        g_remote(c).wait_recv()
        done = set()
        for unit, (dx, dh) in enumerate(UNITS):
            if unit == 5:
                @pl.when(c >= 1)
                def _():
                    stage_pass1(c - 1)

            @pl.when(c == 0)
            def _():
                for dy in (2 * dh, 2 * dh + 1):
                    w_local(dx, dy).wait()
                    w_remote(dx, dy).wait_recv()
            term = jnp.dot(g_all[c], w_all[dx, :, dh * 512:(dh + 1) * 512], preferred_element_type=F32)
            for dy in (2 * dh, 2 * dh + 1):
                for part, dp, dq in ((0, dx, dy), (1, dy, dx)):
                    piece = term[part * SPAN:(part + 1) * SPAN, (dy % 2) * 256:(dy % 2 + 1) * 256]
                    columns = pl.ds((dq % 2) * 256, 256)
                    if dp == 0:
                        own1[part, c, dq // 2, :, columns] = piece
                    else:
                        s1[part, c, dp - 1, dq // 2, :, columns] = piece.astype(BF16)
            for dy in (2 * dh, 2 * dh + 1):
                for part, dp, dq in ((0, dx, dy), (1, dy, dx)):
                    done.add((part, dp, dq))
                    kind = IMMEDIATE.get((dp, dq // 2))
                    if kind is not None and (part, dp, dq ^ 1) in done:
                        first(part, c, kind).start()

    def stage_turn(c):
        for part in (0, 1):
            first(part, c, 2).wait_recv()
            first(part, c, 5).wait_recv()
            total = own1[part, c, 1] + r1n[part, c, 0, 1].astype(F32) + r1n[part, c, 1, 1].astype(F32)
            s2[part, c, 1, 0] = total[:64, :256].astype(BF16)
            second(part, c, 0).start()
            s2[part, c, 1, 1] = total[64:, :256].astype(BF16)
            second(part, c, 1).start()
            s2[part, c, 2, 0] = total[:64, 256:].astype(BF16)
            second(part, c, 3).start()
            s2[part, c, 2, 1] = total[64:, 256:].astype(BF16)
        for part in (0, 1):
            first(part, c, 4).wait_recv()
            first(part, c, 3).wait_recv()
            total = own1[part, c, 0] + r1n[part, c, 0, 0].astype(F32) + r1n[part, c, 1, 0].astype(F32)
            s2[part, c, 0, 1] = total[64:, 256:].astype(BF16)
            second(part, c, 2).start()
            s2[part, c, 0, 0] = total[:64, 256:].astype(BF16)
            acc[part, c] = total[:, :256]

        @pl.when(c == CHUNKS - 1)
        def _():
            for part in (0, 1):
                second(part, c, 4).start()
                second(part, c, 5).start()

    def stage_pass2(c):
        @pl.when(c < CHUNKS - 1)
        def _():
            for part in (0, 1):
                for way, (dp, half) in enumerate(((0, 0), (2, 1))):
                    second(part, c, way).wait_recv()
                    total = s2[part, c, dp, half].astype(F32) + r2o[part, c, way].astype(F32)
                    s2[part, c, dp, half] = total.astype(BF16)
                    second(part, c, 4 + way).start()

    def stage_last(c):
        @pl.when(c == CHUNKS - 1)
        def _():
            for part in (0, 1):
                for half in (0, 1):
                    second(part, c, half).wait_recv()
                    acc[part, c, pl.ds(half * 64, 64)] += r2o[part, c, half].astype(F32)

        for part in (0, 1):
            for half in (0, 1):
                second(part, c, 2 if half else 4).wait_recv()
                second(part, c, 5 if half else 3).wait_recv()
                acc[part, c, pl.ds(half * 64, 64)] += (
                    r2n[part, c, 0, half].astype(F32) + r2n[part, c, 1, half].astype(F32)
                )

    def finish(c):
        for part in (0, 1):
            b = part * CHUNKS + c
            rows = pl.ds(pl.multiple_of(b * SPAN, SPAN), SPAN)
            scale = jnp.sum(jnp.where(square1 == b, scale_v[...], 0.0), axis=1, keepdims=True)
            out[rows, :] = (res[rows, :].astype(F32) + acc[part, c] * scale).astype(BF16)

    def drain_first(c):
        for part in (0, 1):
            for kind in range(6):
                first(part, c, kind).wait_send()
        g_remote(c).wait_send()

    def drain_second(c):
        @pl.when(c < CHUNKS - 1)
        def _():
            for part in (0, 1):
                for kind in range(6):
                    second(part, c, kind).wait_send()

    def drain_rest():
        for dx, dh in UNITS:
            for dy in (2 * dh, 2 * dh + 1):
                w_remote(dx, dy).wait_send()
        for k in range(3):
            req_copy(k).wait_send()
        for i in range(4):
            state_copy(i).wait_send()

    def step(t, _):
        @pl.when(t < CHUNKS - 1)
        def _():
            stage_states(t + 1)

        @pl.when(t < CHUNKS)
        def _():
            stage_project(t)

        @pl.when(t == 2)
        def _():
            ss_in[...] = jnp.transpose(ssa[...])[:8]
            ss_core_copy().start()

        @pl.when(t == 3)
        def _():
            ss_core_copy().wait()
            ss_mid[0] = ss_in[...] + ss_core[...]
            for k in range(3):
                ss_x_copy(k).start()

        @pl.when(t == 4)
        def _():
            for k in range(3):
                ss_x_copy(k).wait()
            ss_mid[1] = ss_mid[0] + ss_x[0] + ss_x[1] + ss_x[2]
            for k in range(3):
                ss_y_copy(k).start()

        @pl.when(t == 4)
        def _():
            drain_rest()

        @pl.when(t == CHUNKS)
        def _():
            stage_pass1(CHUNKS - 1)

        for lag, stage in ((2, stage_turn), (3, stage_pass2), (4, stage_last), (4, drain_first), (5, drain_second)):
            @pl.when(jnp.logical_and(t >= lag, t < CHUNKS + lag))
            def _():
                stage(t - lag)

        @pl.when(t == 5)
        def _():
            for k in range(3):
                ss_y_copy(k).wait()
            loads[5].wait()
            total = ss_mid[1] + ss_y[0] + ss_y[1] + ss_y[2]
            scale = lax.rsqrt(total / 16384.0 + 1e-05)
            scale_v[...] = jnp.transpose(jnp.concatenate([scale] * 16, axis=0))
            finish(0)

        @pl.when(t >= 5)
        def _():
            finish(t - 4)
        return 0

    stage_states(0, True)
    lax.fori_loop(0, CHUNKS + 4, step, 0)

    for part in (0, 1):
        for kind in range(6):
            second(part, CHUNKS - 1, kind).wait_send()


def mixer(owner, slot, spans, decay, bias, skip, x, gate, step, sp, gain, w, res, cache):
    vmem = pl.BlockSpec(memory_space=pltpu.VMEM)
    hbm = pl.BlockSpec(memory_space=pl.ANY)
    dma = pltpu.SemaphoreType.DMA
    return pl.pallas_call(
        mixer_kernel,
        out_shape=(
            pltpu.VMEM(res.shape, res.dtype),
            pltpu.VMEM((2, 512, 256), F32),
        ),
        in_specs=[hbm] * 14,
        out_specs=(vmem, vmem),
        scratch_shapes=[
            pltpu.SMEM((2, 8), I32),
            pltpu.SMEM((2, 8), I32),
            pltpu.SMEM((2,), I32),
            pltpu.SMEM((8,), F32),
            pltpu.SMEM((8,), F32),
            pltpu.SMEM((8,), F32),
            pltpu.VMEM((1024, 512), BF16),
            pltpu.VMEM((1024, 512), BF16),
            pltpu.VMEM((8, 1024), F32),
            pltpu.VMEM((8, 2, 1024, 256), BF16),
            pltpu.VMEM((1, 512), F32),
            pltpu.VMEM((1024, 256), BF16),
            pltpu.VMEM((64, 64, 256), BF16),
            pltpu.VMEM((8, 128), I32),
            pltpu.VMEM((3, 8, 128), I32),
            pltpu.SMEM((3, 8, 128), I32),
            pltpu.SMEM((3, 16), I32),
            pltpu.VMEM((18, 64, 256), BF16),
            pltpu.VMEM((18, 64, 256), BF16),
            pltpu.VMEM((2, 3, 64, 256), BF16),
            pltpu.VMEM((64, 128), F32),
            pltpu.VMEM((64, 128), F32),
            pltpu.VMEM((64, 128), F32),
            pltpu.VMEM((128, 1024), BF16),
            pltpu.VMEM((8, 128, 512), F32),
            pltpu.VMEM((8, 128, 512), F32),
            pltpu.VMEM((8, 128, 512), F32),
            pltpu.VMEM((8, 512, 256), F32),
            pltpu.VMEM((8, 128, 256), BF16),
            pltpu.VMEM((2, 512, 256), BF16),
            pltpu.VMEM((128, 128), F32),
            pltpu.VMEM((8, 128), F32),
            pltpu.VMEM((4, 1024, 1024), BF16),
            pltpu.VMEM((4, 256, 1024), BF16),
            pltpu.VMEM((128, 128), F32),
            pltpu.VMEM((2, 4, 3, 2, 128, 512), BF16),
            pltpu.VMEM((2, 4, 2, 128, 512), F32),
            pltpu.VMEM((2, 4, 2, 128, 512), BF16),
            pltpu.VMEM((2, 4, 2, 2, 128, 512), BF16),
            pltpu.VMEM((2, 4, 3, 2, 64, 256), BF16),
            pltpu.VMEM((2, 4, 128, 256), F32),
            pltpu.VMEM((2, 4, 2, 64, 256), BF16),
            pltpu.VMEM((2, 4, 2, 2, 64, 256), BF16),
            pltpu.VMEM((2, 8, 128), F32),
            pltpu.VMEM((8, 128), F32),
            pltpu.VMEM((3, 8, 128), F32),
            pltpu.VMEM((3, 8, 128), F32),
            dma((6,)), dma((8,)), dma((3,)), dma((3,)), dma((3,)), dma((4,)), dma((4,)), dma((6,)),
            dma((4, 4)), dma((4, 4)), dma((4, 4)), dma((4,)), dma((4,)),
            dma((2, 4, 6)), dma((2, 4, 6)), dma((2, 4, 6)), dma((2, 4, 6)),
            dma((7,)), dma((7,)),
        ],
        compiler_params=pltpu.CompilerParams(
            collective_id=0, has_side_effects=True, vmem_limit_bytes=61 * 1024 * 1024
        ),
        cost_estimate=pl.CostEstimate(flops=10000000000, bytes_accessed=24000000, transcendentals=0),
        name="mixer",
    )(owner, slot, spans, decay, bias, skip, x, gate, step, sp, gain, w, res, cache)


def emit_kernel(mixed, state, mixed_out, state_out, sems):
    copies = []
    for i in range(4):
        rows = pl.ds(i * 256, 256)
        copies.append(pltpu.make_async_copy(mixed.at[rows], mixed_out.at[rows], sems.at[i]))
        rows = pl.ds((i % 2) * 256, 256)
        copies.append(pltpu.make_async_copy(state.at[i // 2, rows], state_out.at[i // 2, rows], sems.at[4 + i]))
    for copy in copies:
        copy.start()
    for copy in copies:
        copy.wait()


def emit(mixed, state):
    vmem = pl.BlockSpec(memory_space=pltpu.VMEM)
    hbm = pl.BlockSpec(memory_space=pl.ANY)
    return pl.pallas_call(
        emit_kernel,
        out_shape=(
            jax.ShapeDtypeStruct(mixed.shape, mixed.dtype),
            jax.ShapeDtypeStruct(state.shape, state.dtype),
        ),
        in_specs=[vmem] * 2,
        out_specs=(hbm, hbm),
        scratch_shapes=[pltpu.SemaphoreType.DMA((8,))],
        compiler_params=pltpu.CompilerParams(vmem_limit_bytes=4 * 1024 * 1024),
        name="emit",
    )(mixed, state)


def per_device(
    mixer_input, gate_input, step_raw, state_proj, decay_log, step_bias, skip_gain, norm_gain,
    out_weight, residual, new_spans, hit_owner, hit_slot, state_cache,
):
    mixed, final = mixer(
        hit_owner, hit_slot, new_spans, decay_log, step_bias, skip_gain,
        mixer_input, gate_input, step_raw.T, state_proj.reshape(2, 8192, 256),
        norm_gain.reshape(1, 512), out_weight, residual, state_cache.reshape(64, 64, 256),
    )
    mixed, final = emit(mixed, final)
    return mixed, final.reshape(2, 8, 64, 256)


def solution(mesh):
    in_specs = (
        P("group", "head"),
        P("group", "head"),
        P("group", "head"),
        P(None, "group", None, None),
        P("head"),
        P("head"),
        P("head"),
        P("head"),
        P("head", None),
        P("group", "head"),
        P("group"),
        P("group", "head"),
        P("group", "head"),
        P("group", "head", None, None),
    )
    out_specs = (P("group", "head"), P("group", "head", None, None))
    return jax.shard_map(
        per_device, mesh=mesh, in_specs=in_specs, out_specs=out_specs, check_vma=False
    )
```

```python
import jax
import jax.numpy as jnp
from jax import lax
from jax.experimental import pallas as pl
from jax.experimental.pallas import tpu as pltpu
from jax.sharding import PartitionSpec as P

SPAN = 128
CAP = 6
UNITS = ((2, 1), (2, 0), (3, 1), (3, 0), (1, 1), (0, 1), (1, 0), (0, 0))
SIDE = 4
CHUNKS = 4
WEIGHTS_FIRST = False
BLOCKS = 8
MESH = pl.DeviceIdType.MESH
BF16 = jnp.bfloat16
F32 = jnp.float32
I32 = jnp.int32
HIGHEST = lax.Precision.HIGHEST


def remote(src, dst, send_sem, recv_sem, where):
    return pltpu.make_async_remote_copy(
        src_ref=src, dst_ref=dst, send_sem=send_sem, recv_sem=recv_sem,
        device_id=where, device_id_type=MESH,
    )


def dot_tn(a, b):
    return lax.dot_general(a, b, (((0,), (0,)), ((), ())), preferred_element_type=F32)


def dot_nt(a, b):
    return lax.dot_general(a, b, (((1,), (1,)), ((), ())), preferred_element_type=F32)


def mixer_kernel(
    owner_hbm, slot_hbm, spans_hbm, decay_hbm, bias_hbm, skip_hbm,
    x_hbm, gate_hbm, step_hbm, sp_hbm, gain_hbm, w_hbm, res_hbm, cache_hbm,
    out, h_v,
    owner_s, slot_s, spans_s, decay_s, bias_s, skip_s,
    x_v, gate_v, step_v, sp_v, gain_v, res, cache_v,
    req_v, rreq, req_s, idx_s, pbuf, rbuf, relay,
    e_v, f_v, em_v, sel_v, yi_v, silu_v, ee_v, u_v, c_v, hb_v, ssa, ss_in,
    w_all, g_all, scale_v, s1, own1, r1o, r1n, s2, acc, r2o, r2n,
    ss_mid, ss_core, ss_x, ss_y,
    sem_in, sem_sp, sem_req_s, sem_req_r, sem_rs, sem_st_s, sem_st_r, sem_sc,
    sem_w, sem_ws, sem_wr, sem_gs, sem_gr, sem_1s, sem_1r, sem_2s, sem_2r, sem_ss, sem_sr,
):
    me = lax.axis_index("head")
    deep = lax.axis_index("group")
    core = lax.rem(me, 2)
    col = lax.rem(me // 2, SIDE)
    row = me // (2 * SIDE)

    def head_at(dx, dy, dc):
        y = lax.rem(row + dy, SIDE)
        x = lax.rem(col + dx, SIDE)
        c = lax.rem(core + dc, 2)
        return (y * SIDE + x) * 2 + c

    def at_head(h):
        return {"head": h}

    partner = at_head(head_at(0, 0, 1))
    x_peers = [at_head(head_at(k, 0, 0)) for k in (1, 2, 3)]
    y_peers = [at_head(head_at(0, k, 0)) for k in (1, 2, 3)]
    z_peers = [{"group": lax.rem(deep + k, 4)} for k in (1, 2, 3)]
    p_side = ((x_peers[0], x_peers[2]), (y_peers[0], y_peers[2]))
    q_side = (p_side[1], p_side[0])

    barrier = pltpu.get_barrier_semaphore()
    for peer in z_peers + [partner] + x_peers + y_peers:
        pl.semaphore_signal(barrier, inc=1, device_id=peer, device_id_type=MESH)

    loads = [
        pltpu.make_async_copy(src, dst, sem_in.at[i])
        for i, (src, dst) in enumerate((
            (cache_hbm, cache_v), (step_hbm, step_v), (x_hbm, x_v), (gain_hbm, gain_v),
            (gate_hbm, gate_v), (res_hbm, res),
        ))
    ]

    def sp_copy(b):
        start = pl.multiple_of(b * 1024, 1024)
        return pltpu.make_async_copy(sp_hbm.at[:, pl.ds(start, 1024)], sp_v.at[b], sem_sp.at[b])

    def w_local(dx, dy):
        start = pl.multiple_of(head_at(dx, dy, 0) * 256, 256)
        dst = w_all.at[dx, pl.ds(0, 512), pl.ds(dy * 256, 256)]
        return pltpu.make_async_copy(w_hbm.at[:, pl.ds(start, 256)], dst, sem_w.at[dx, dy])

    def w_remote(dx, dy):
        start = pl.multiple_of(head_at(dx, dy, 1) * 256, 256)
        dst = w_all.at[dx, pl.ds(512, 512), pl.ds(dy * 256, 256)]
        return remote(w_hbm.at[:, pl.ds(start, 256)], dst, sem_ws.at[dx, dy], sem_wr.at[dx, dy], partner)

    def start_weights():
        for dx, dh in UNITS:
            for dy in (2 * dh, 2 * dh + 1):
                w_remote(dx, dy).start()
                w_local(dx, dy).start()
        loads[5].start()

    def g_remote(c):
        return remote(
            g_all.at[c, :, pl.ds(0, 512)], g_all.at[c, :, pl.ds(512, 512)], sem_gs.at[c], sem_gr.at[c], partner
        )

    scalars = [
        pltpu.make_async_copy(src, dst, sem_sc.at[i])
        for i, (src, dst) in enumerate((
            (owner_hbm, owner_s), (slot_hbm, slot_s), (spans_hbm, spans_s),
            (decay_hbm, decay_s), (bias_hbm, bias_s), (skip_hbm, skip_s),
        ))
    ]
    for scalar in scalars:
        scalar.start()
    for load in loads[:5]:
        load.start()
    for b in range(BLOCKS):
        sp_copy(b).start()

    for scalar in scalars[:2]:
        scalar.wait()

    lane = lax.broadcasted_iota(I32, (8, 128), 1)
    lane_owner = lane // 8
    lane_rank = lane % 8
    request = jnp.zeros((8, 128), I32)
    for e in range(16):
        s, j = divmod(e, 8)
        named = lane_owner == owner_s[s, j]
        request = jnp.where(jnp.logical_and(named, lane_rank == 0), slot_s[s, j] * 8 + j, request)
        lane_rank = lane_rank - jnp.where(named, 1, 0)
    req_v[...] = request

    def req_copy(k):
        return remote(req_v, rreq.at[k], sem_req_s.at[k], sem_req_r.at[k], z_peers[k])

    pl.semaphore_wait(barrier, 10)
    for k in (0, 2, 1):
        req_copy(k).start()
    if WEIGHTS_FIRST:
        start_weights()

    for scalar in scalars[2:]:
        scalar.wait()

    sub = lax.broadcasted_iota(I32, (8, 128), 0)
    bias = jnp.zeros((8, 128), F32)
    decay = jnp.zeros((8, 128), F32)
    for j in range(8):
        bias = jnp.where(sub == j, bias_s[j], bias)
        decay = jnp.where(sub == j, decay_s[j], decay)
    decay = -jnp.exp(decay)
    loads[1].wait()
    steps = []
    for b in range(BLOCKS):
        raw = step_v[:, b * SPAN:(b + 1) * SPAN] + bias
        alive = jnp.where(b % CHUNKS < spans_s[b // CHUNKS], 1.0, 0.0)
        steps.append((jnp.maximum(raw, 0.0) + jnp.log1p(jnp.exp(-jnp.abs(raw)))) * alive)
    dt = jnp.concatenate(steps, axis=0)
    rate = jnp.concatenate([decay * step for step in steps], axis=0)
    square0 = lax.broadcasted_iota(I32, (SPAN, SPAN), 0)
    square1 = lax.broadcasted_iota(I32, (SPAN, SPAN), 1)
    upper = jnp.where(square0 <= square1, 1.0, 0.0).astype(F32)
    cum = jnp.dot(rate, upper, precision=HIGHEST, preferred_element_type=F32)
    middle = cum[:, SPAN - 1:] * 0.5
    e_v[...] = jnp.exp(cum - middle)
    f_v[...] = jnp.exp(middle - cum) * dt
    em_v[...] = jnp.exp(jnp.broadcast_to(middle, (BLOCKS * 8, 128)))
    ssa[...] = jnp.zeros((SPAN, SPAN), F32)

    def state_copy(i):
        src, dst, way = (
            (pbuf.at[pl.ds(6, 3)], rbuf.at[pl.ds(6, 3)], 1),
            (pbuf.at[pl.ds(9, 3)], rbuf.at[pl.ds(9, 3)], 1),
            (pbuf.at[pl.ds(0, 6)], rbuf.at[pl.ds(0, 6)], 2),
            (pbuf.at[pl.ds(12, 6)], rbuf.at[pl.ds(12, 6)], 0),
        )[i]
        return remote(src, dst, sem_st_s.at[i], sem_st_r.at[i], z_peers[way])

    loads[0].wait()
    for k in (0, 2, 1):
        req_copy(k).wait_recv()
        list_k = rreq[k]
        for r in range(CAP):
            place = jnp.sum(jnp.where(lane[:1] == deep * 8 + r, list_k[:1], 0))
            pbuf[k * CAP + r] = cache_v[place]
            if k == 1 and r == 2:
                state_copy(0).start()
        state_copy((2, 1, 3)[k]).start()
    if not WEIGHTS_FIRST:
        start_weights()

    counts = [jnp.int32(0)] * 4
    for e in range(16):
        s, j = divmod(e, 8)
        owner = owner_s[s, j]
        rank = jnp.int32(0)
        for q in range(4):
            rank = jnp.where(owner == q, counts[q], rank)
            counts[q] = counts[q] + jnp.where(owner == q, 1, 0)
        away = lax.rem(owner - deep + 4, 4)
        idx_s[0, e] = jnp.where(away == 0, 0, (away - 1) * CAP + jnp.minimum(rank, CAP - 1))
        idx_s[1, e] = jnp.where(away == 0, 1, 0)
        idx_s[2, e] = slot_s[s, j] * 8 + j

    pick = me // 4
    sel_v[...] = jnp.where(
        lax.broadcasted_iota(I32, (SPAN, 1024), 1) == lax.broadcasted_iota(I32, (SPAN, 1024), 0) * 8 + pick, 1.0, 0.0
    ).astype(BF16)
    channel = lax.broadcasted_iota(I32, (16, 512), 1)
    spread = jnp.where(channel // 64 == lax.broadcasted_iota(I32, (16, 512), 0) % 8, 1.0, 0.0).astype(BF16)
    channel = lax.broadcasted_iota(I32, (1, 512), 1)
    skip = jnp.zeros((1, 512), F32)
    for j in range(8):
        skip = jnp.where(channel // 64 == j, skip_s[j], skip)
    for load in loads[2:5]:
        load.wait()

    def widen(part):
        high = part.astype(BF16)
        low = (part - high.astype(F32)).astype(BF16)
        return dot_tn(jnp.concatenate([high, low], axis=0), spread)

    def prepare(b, _):
        sp_copy(b).wait()
        few = pl.ds(pl.multiple_of(b * 8, 8), 8)
        x = x_v[pl.ds(pl.multiple_of(b * SPAN, SPAN), SPAN), :].astype(F32)
        wide_e = widen(e_v[few, :])
        ee_v[b] = wide_e
        z = (widen(f_v[few, :]) * x).astype(BF16)
        b_rows = jnp.dot(sel_v[...], sp_v[b, 0], preferred_element_type=F32).astype(BF16)
        c_rows = jnp.dot(sel_v[...], sp_v[b, 1], preferred_element_type=F32).astype(BF16)
        c_v[b] = c_rows
        scores = jnp.where(square0 >= square1, dot_nt(c_rows, b_rows), 0.0).astype(BF16)
        yi_v[b] = wide_e * jnp.dot(scores, z, preferred_element_type=F32) + skip * x
        u_v[b] = dot_tn(z, b_rows)
        gate = gate_v[pl.ds(pl.multiple_of(b * SPAN, SPAN), SPAN), :].astype(F32)
        silu_v[b] = gate / (1.0 + jnp.exp(-gate))
        return 0

    lax.fori_loop(0, BLOCKS, prepare, 0)

    def fade_of(b, j):
        fade = em_v[pl.ds(b * 8 + j, 1), :]
        return jnp.concatenate([fade, fade], axis=1)

    for i in (0, 1, 2, 3):
        state_copy(i).wait_recv()
    for e in range(16):
        s, j = divmod(e, 8)
        here = cache_v[idx_s[2, e]].astype(F32)
        sent = rbuf[idx_s[0, e]].astype(F32)
        state = jnp.where(idx_s[1, e] == 1, here, sent)
        rows = slice(j * 64, (j + 1) * 64)
        h_v[s, rows, :] = state
        hb_v[s, rows, :] = (state * fade_of(s * CHUNKS, j)).astype(BF16)

    def stage_states(c, fresh=False):
        for s in (0, 1):
            b = s * CHUNKS + c
            for j in range(0 if fresh else 8):
                rows = slice(j * 64, (j + 1) * 64)
                hb_v[s, rows, :] = (h_v[s, rows, :] * fade_of(b, j)).astype(BF16)
            y = yi_v[b] + ee_v[b] * dot_nt(c_v[b], hb_v[s])
            gated = y * silu_v[b]
            g_all[c, s * SPAN:(s + 1) * SPAN, :512] = (gated * gain_v[...]).astype(BF16)
            yi_v[b] = gated
        g_remote(c).start()
        for s in (0, 1):
            b = s * CHUNKS + c
            gated = yi_v[b]
            ssa[...] = jnp.where(square1 == b, jnp.sum(gated * gated, axis=1, keepdims=True), ssa[...])
            for j in range(8):
                rows = slice(j * 64, (j + 1) * 64)
                fade = fade_of(b, j)
                h_v[s, rows, :] = (h_v[s, rows, :] * fade + u_v[b, rows, :]) * fade


    def ss_core_copy():
        return remote(ss_in, ss_core, sem_ss.at[0], sem_sr.at[0], partner)

    def ss_x_copy(k):
        return remote(ss_mid.at[0], ss_x.at[k], sem_ss.at[1 + k], sem_sr.at[1 + k], x_peers[k])

    def ss_y_copy(k):
        return remote(ss_mid.at[1], ss_y.at[k], sem_ss.at[4 + k], sem_sr.at[4 + k], y_peers[k])

    def first(part, c, kind):
        if kind == 0:
            src, dst, way = s1.at[part, c, 1, 0], r1o.at[part, c, 0], 0
        elif kind == 1:
            src, dst, way = s1.at[part, c, 1, 1], r1o.at[part, c, 1], 1
        elif kind == 2:
            src, dst, way = s1.at[part, c, 0, 1], r1n.at[part, c, 0, 1], 0
        elif kind == 3:
            src, dst, way = s1.at[part, c, 2, 0], r1n.at[part, c, 1, 0], 1
        elif kind == 4:
            src, dst, way = s1.at[part, c, 0, 0], r1n.at[part, c, 0, 0], 0
        else:
            src, dst, way = s1.at[part, c, 2, 1], r1n.at[part, c, 1, 1], 1
        return remote(src, dst, sem_1s.at[part, c, kind], sem_1r.at[part, c, kind], p_side[part][way])

    def second_to(part, c, way):
        if way < 2:
            return q_side[part][way]
        near = q_side[part][way - 2]["head"]
        far = (y_peers, x_peers)[part][1]["head"]
        return at_head(jnp.where(c == CHUNKS - 1, far, near))

    def second(part, c, kind):
        if kind == 0:
            src, dst, way = s2.at[part, c, 1, 0], r2o.at[part, c, 0], 2
        elif kind == 1:
            src, dst, way = s2.at[part, c, 1, 1], r2o.at[part, c, 1], 3
        elif kind == 2:
            src, dst, way = s2.at[part, c, 0, 1], r2n.at[part, c, 0, 1], 0
        elif kind == 3:
            src, dst, way = s2.at[part, c, 2, 0], r2n.at[part, c, 1, 0], 1
        elif kind == 4:
            src, dst, way = s2.at[part, c, 0, 0], r2n.at[part, c, 0, 0], 0
        else:
            src, dst, way = s2.at[part, c, 2, 1], r2n.at[part, c, 1, 1], 1
        return remote(src, dst, sem_2s.at[part, c, kind], sem_2r.at[part, c, kind], second_to(part, c, way))

    IMMEDIATE = {(2, 0): 0, (2, 1): 1, (1, 1): 2, (3, 0): 3}

    def stage_pass1(c):
        for part in (0, 1):
            for way, (dp, half) in enumerate(((0, 0), (2, 1))):
                first(part, c, way).wait_recv()
                total = s1[part, c, dp, half].astype(F32) + r1o[part, c, way].astype(F32)
                s1[part, c, dp, half] = total.astype(BF16)
                first(part, c, 4 + way).start()

    def stage_project(c):
        g_remote(c).wait_recv()
        done = set()
        for unit, (dx, dh) in enumerate(UNITS):
            if unit == 4:
                @pl.when(c >= 1)
                def _():
                    stage_pass1(c - 1)

            @pl.when(c == 0)
            def _():
                for dy in (2 * dh, 2 * dh + 1):
                    w_local(dx, dy).wait()
                    w_remote(dx, dy).wait_recv()
            term = jnp.dot(g_all[c], w_all[dx, :, dh * 512:(dh + 1) * 512], preferred_element_type=F32)
            for dy in (2 * dh, 2 * dh + 1):
                for part, dp, dq in ((0, dx, dy), (1, dy, dx)):
                    piece = term[part * SPAN:(part + 1) * SPAN, (dy % 2) * 256:(dy % 2 + 1) * 256]
                    columns = pl.ds((dq % 2) * 256, 256)
                    if dp == 0:
                        own1[part, c, dq // 2, :, columns] = piece
                    else:
                        s1[part, c, dp - 1, dq // 2, :, columns] = piece.astype(BF16)
            for dy in (2 * dh, 2 * dh + 1):
                for part, dp, dq in ((0, dx, dy), (1, dy, dx)):
                    done.add((part, dp, dq))
                    kind = IMMEDIATE.get((dp, dq // 2))
                    if kind is not None and (part, dp, dq ^ 1) in done:
                        first(part, c, kind).start()

    def stage_turn(c):
        for part in (0, 1):
            first(part, c, 2).wait_recv()
            first(part, c, 5).wait_recv()
            total = own1[part, c, 1] + r1n[part, c, 0, 1].astype(F32) + r1n[part, c, 1, 1].astype(F32)
            s2[part, c, 1, 0] = total[:64, :256].astype(BF16)
            second(part, c, 0).start()
            s2[part, c, 1, 1] = total[64:, :256].astype(BF16)
            second(part, c, 1).start()
            s2[part, c, 2, 0] = total[:64, 256:].astype(BF16)
            second(part, c, 3).start()
            s2[part, c, 2, 1] = total[64:, 256:].astype(BF16)
        for part in (0, 1):
            first(part, c, 4).wait_recv()
            first(part, c, 3).wait_recv()
            total = own1[part, c, 0] + r1n[part, c, 0, 0].astype(F32) + r1n[part, c, 1, 0].astype(F32)
            s2[part, c, 0, 1] = total[64:, 256:].astype(BF16)
            second(part, c, 2).start()
            s2[part, c, 0, 0] = total[:64, 256:].astype(BF16)
            acc[part, c] = total[:, :256]

        @pl.when(c == CHUNKS - 1)
        def _():
            for part in (0, 1):
                second(part, c, 4).start()
                second(part, c, 5).start()

    def stage_pass2(c):
        @pl.when(c < CHUNKS - 1)
        def _():
            for part in (0, 1):
                for way, (dp, half) in enumerate(((0, 0), (2, 1))):
                    second(part, c, way).wait_recv()
                    total = s2[part, c, dp, half].astype(F32) + r2o[part, c, way].astype(F32)
                    s2[part, c, dp, half] = total.astype(BF16)
                    second(part, c, 4 + way).start()

    def stage_last(c):
        @pl.when(c == CHUNKS - 1)
        def _():
            for part in (0, 1):
                for half in (0, 1):
                    second(part, c, half).wait_recv()
                    acc[part, c, pl.ds(half * 64, 64)] += r2o[part, c, half].astype(F32)

        for part in (0, 1):
            for half in (0, 1):
                second(part, c, 2 if half else 4).wait_recv()
                second(part, c, 5 if half else 3).wait_recv()
                acc[part, c, pl.ds(half * 64, 64)] += (
                    r2n[part, c, 0, half].astype(F32) + r2n[part, c, 1, half].astype(F32)
                )

    def finish(c):
        for part in (0, 1):
            b = part * CHUNKS + c
            rows = pl.ds(pl.multiple_of(b * SPAN, SPAN), SPAN)
            scale = jnp.sum(jnp.where(square1 == b, scale_v[...], 0.0), axis=1, keepdims=True)
            out[rows, :] = (res[rows, :].astype(F32) + acc[part, c] * scale).astype(BF16)

    def drain_first(c):
        for part in (0, 1):
            for kind in range(6):
                first(part, c, kind).wait_send()
        g_remote(c).wait_send()

    def drain_second(c):
        @pl.when(c < CHUNKS - 1)
        def _():
            for part in (0, 1):
                for kind in range(6):
                    second(part, c, kind).wait_send()

    def drain_rest():
        for dx, dh in UNITS:
            for dy in (2 * dh, 2 * dh + 1):
                w_remote(dx, dy).wait_send()
        for k in range(3):
            req_copy(k).wait_send()
        for i in range(4):
            state_copy(i).wait_send()

    def step(t, _):
        @pl.when(t < CHUNKS - 1)
        def _():
            stage_states(t + 1)

        @pl.when(t < CHUNKS)
        def _():
            stage_project(t)

        @pl.when(t == 2)
        def _():
            ss_in[...] = jnp.transpose(ssa[...])[:8]
            ss_core_copy().start()

        @pl.when(t == 3)
        def _():
            ss_core_copy().wait()
            ss_mid[0] = ss_in[...] + ss_core[...]
            for k in range(3):
                ss_x_copy(k).start()

        @pl.when(t == 4)
        def _():
            for k in range(3):
                ss_x_copy(k).wait()
            ss_mid[1] = ss_mid[0] + ss_x[0] + ss_x[1] + ss_x[2]
            for k in range(3):
                ss_y_copy(k).start()

        @pl.when(t == 4)
        def _():
            drain_rest()

        @pl.when(t == CHUNKS)
        def _():
            stage_pass1(CHUNKS - 1)

        for lag, stage in ((2, stage_turn), (3, stage_pass2), (4, stage_last), (4, drain_first), (5, drain_second)):
            @pl.when(jnp.logical_and(t >= lag, t < CHUNKS + lag))
            def _():
                stage(t - lag)

        @pl.when(t == 5)
        def _():
            for k in range(3):
                ss_y_copy(k).wait()
            loads[5].wait()
            total = ss_mid[1] + ss_y[0] + ss_y[1] + ss_y[2]
            scale = lax.rsqrt(total / 16384.0 + 1e-05)
            scale_v[...] = jnp.transpose(jnp.concatenate([scale] * 16, axis=0))
            finish(0)

        @pl.when(t >= 5)
        def _():
            finish(t - 4)
        return 0

    stage_states(0, True)
    lax.fori_loop(0, CHUNKS + 4, step, 0)

    for part in (0, 1):
        for kind in range(6):
            second(part, CHUNKS - 1, kind).wait_send()


def mixer(owner, slot, spans, decay, bias, skip, x, gate, step, sp, gain, w, res, cache):
    vmem = pl.BlockSpec(memory_space=pltpu.VMEM)
    hbm = pl.BlockSpec(memory_space=pl.ANY)
    dma = pltpu.SemaphoreType.DMA
    return pl.pallas_call(
        mixer_kernel,
        out_shape=(
            pltpu.VMEM(res.shape, res.dtype),
            pltpu.VMEM((2, 512, 256), F32),
        ),
        in_specs=[hbm] * 14,
        out_specs=(vmem, vmem),
        scratch_shapes=[
            pltpu.SMEM((2, 8), I32),
            pltpu.SMEM((2, 8), I32),
            pltpu.SMEM((2,), I32),
            pltpu.SMEM((8,), F32),
            pltpu.SMEM((8,), F32),
            pltpu.SMEM((8,), F32),
            pltpu.VMEM((1024, 512), BF16),
            pltpu.VMEM((1024, 512), BF16),
            pltpu.VMEM((8, 1024), F32),
            pltpu.VMEM((8, 2, 1024, 256), BF16),
            pltpu.VMEM((1, 512), F32),
            pltpu.VMEM((1024, 256), BF16),
            pltpu.VMEM((64, 64, 256), BF16),
            pltpu.VMEM((8, 128), I32),
            pltpu.VMEM((3, 8, 128), I32),
            pltpu.SMEM((3, 8, 128), I32),
            pltpu.SMEM((3, 16), I32),
            pltpu.VMEM((18, 64, 256), BF16),
            pltpu.VMEM((18, 64, 256), BF16),
            pltpu.VMEM((2, 3, 64, 256), BF16),
            pltpu.VMEM((64, 128), F32),
            pltpu.VMEM((64, 128), F32),
            pltpu.VMEM((64, 128), F32),
            pltpu.VMEM((128, 1024), BF16),
            pltpu.VMEM((8, 128, 512), F32),
            pltpu.VMEM((8, 128, 512), F32),
            pltpu.VMEM((8, 128, 512), F32),
            pltpu.VMEM((8, 512, 256), F32),
            pltpu.VMEM((8, 128, 256), BF16),
            pltpu.VMEM((2, 512, 256), BF16),
            pltpu.VMEM((128, 128), F32),
            pltpu.VMEM((8, 128), F32),
            pltpu.VMEM((4, 1024, 1024), BF16),
            pltpu.VMEM((4, 256, 1024), BF16),
            pltpu.VMEM((128, 128), F32),
            pltpu.VMEM((2, 4, 3, 2, 128, 512), BF16),
            pltpu.VMEM((2, 4, 2, 128, 512), F32),
            pltpu.VMEM((2, 4, 2, 128, 512), BF16),
            pltpu.VMEM((2, 4, 2, 2, 128, 512), BF16),
            pltpu.VMEM((2, 4, 3, 2, 64, 256), BF16),
            pltpu.VMEM((2, 4, 128, 256), F32),
            pltpu.VMEM((2, 4, 2, 64, 256), BF16),
            pltpu.VMEM((2, 4, 2, 2, 64, 256), BF16),
            pltpu.VMEM((2, 8, 128), F32),
            pltpu.VMEM((8, 128), F32),
            pltpu.VMEM((3, 8, 128), F32),
            pltpu.VMEM((3, 8, 128), F32),
            dma((6,)), dma((8,)), dma((3,)), dma((3,)), dma((3,)), dma((4,)), dma((4,)), dma((6,)),
            dma((4, 4)), dma((4, 4)), dma((4, 4)), dma((4,)), dma((4,)),
            dma((2, 4, 6)), dma((2, 4, 6)), dma((2, 4, 6)), dma((2, 4, 6)),
            dma((7,)), dma((7,)),
        ],
        compiler_params=pltpu.CompilerParams(
            collective_id=0, has_side_effects=True, vmem_limit_bytes=61 * 1024 * 1024
        ),
        cost_estimate=pl.CostEstimate(flops=10000000000, bytes_accessed=24000000, transcendentals=0),
        name="mixer",
    )(owner, slot, spans, decay, bias, skip, x, gate, step, sp, gain, w, res, cache)


def emit_kernel(mixed, state, mixed_out, state_out, sems):
    copies = [
        pltpu.make_async_copy(state, state_out, sems.at[0]),
        pltpu.make_async_copy(mixed, mixed_out, sems.at[1]),
    ]
    for copy in copies:
        copy.start()
    for copy in copies:
        copy.wait()


def emit(mixed, state):
    vmem = pl.BlockSpec(memory_space=pltpu.VMEM)
    hbm = pl.BlockSpec(memory_space=pl.ANY)
    return pl.pallas_call(
        emit_kernel,
        out_shape=(
            jax.ShapeDtypeStruct(mixed.shape, mixed.dtype),
            jax.ShapeDtypeStruct(state.shape, state.dtype),
        ),
        in_specs=[vmem] * 2,
        out_specs=(hbm, hbm),
        scratch_shapes=[pltpu.SemaphoreType.DMA((8,))],
        compiler_params=pltpu.CompilerParams(vmem_limit_bytes=4 * 1024 * 1024),
        name="emit",
    )(mixed, state)


def per_device(
    mixer_input, gate_input, step_raw, state_proj, decay_log, step_bias, skip_gain, norm_gain,
    out_weight, residual, new_spans, hit_owner, hit_slot, state_cache,
):
    mixed, final = mixer(
        hit_owner, hit_slot, new_spans, decay_log, step_bias, skip_gain,
        mixer_input, gate_input, step_raw.T, state_proj.reshape(2, 8192, 256),
        norm_gain.reshape(1, 512), out_weight, residual, state_cache.reshape(64, 64, 256),
    )
    mixed, final = emit(mixed, final)
    return mixed, final.reshape(2, 8, 64, 256)


def solution(mesh):
    in_specs = (
        P("group", "head"),
        P("group", "head"),
        P("group", "head"),
        P(None, "group", None, None),
        P("head"),
        P("head"),
        P("head"),
        P("head"),
        P("head", None),
        P("group", "head"),
        P("group"),
        P("group", "head"),
        P("group", "head"),
        P("group", "head", None, None),
    )
    out_specs = (P("group", "head"), P("group", "head", None, None))
    return jax.shard_map(
        per_device, mesh=mesh, in_specs=in_specs, out_specs=out_specs, check_vma=False
    )
```
